256 devices in a mesh: seq: 64 (over y, x_hi, z), head: 4 (over x_lo, core).
Axes of the slice: x: 4 (x_hi: 2, x_lo: 2; x = x_hi * 2 + x_lo), y: 4, z: 8, core: 2. Of those that a mesh axis runs over, the one named last changes fastest.
Arguments:
- video_query: bfloat16 [8192, 2560], P('seq', 'head'), may hold values from -1800 to 1800
- video_key: bfloat16 [8192, 2560], P('seq', 'head'), may hold values from -1800 to 1800
- video_value: bfloat16 [8192, 2560], P('seq', 'head'), may hold values from -6 to 6
- cross_query: bfloat16 [8192, 2560], P('seq', 'head'), may hold values from -1800 to 1800
- text_key: bfloat16 [512, 2560], P('seq', 'head'), may hold values from -1800 to 1800
- text_value: bfloat16 [512, 2560], P('seq', 'head'), may hold values from -6 to 6
- text_mask: int32 [512], P('seq'), may hold values from 0 to 1, as said below
- norm_gains: float32 [4, 2560], P(None, 'head'), may hold values from 0.8 to 2.5
- gate_table: float32 [1000, 2560], P(None, 'head'), may hold values from -4 to 4
- timestep: int32 [1], replicated, may hold values from 0 to 999
Outputs:
- block_update: bfloat16 [8192, 2560], P('seq', 'head')
The draws below stay inside these ranges and needn't reach their ends.
Inputs may be any that keep to these rules, and one draw needn't show every extreme that they name: `text_mask`: the ones form a prefix of at least 64 positions, zeros follow.
All inputs are finite; a program needn't handle non-finite values.
Results may differ from the reference program's by a relative error of at most 0.0055.
The reference program's roundings to bfloat16 on the way count: a program that leaves them out, or rounds other values in their place, can miss the bound.
Values may be sent and summed in bfloat16 or wider, within the bound.
No kernel may reach another device: no remote copies, remote signals or barrier semaphores. Data moves between devices by JAX's collectives and lax.ppermute only.
A program may use at most 128 MiB of HBM per device.

```python
import math
import jax
import jax.numpy as jnp
from jax import lax

HEADS = 20
HD = 128
TEXT = 512
STEPS = 1000
TOKENS = 8192


def scale_grid(key, row_total, col_total):
    first, second = jax.random.split(key)
    row_part = 10.0 ** jax.random.uniform(first, (row_total, 1))
    ramp = 3.0 ** (jnp.arange(col_total, dtype=jnp.float32) / col_total)
    col_part = 10.0 ** jax.random.uniform(second, (1, col_total)) * ramp[None, :]
    return row_part * col_part


def base_entries(key, row_total):
    first, second = jax.random.split(key)
    entries = jnp.clip(jax.random.normal(first, (row_total, HEADS * HD)), -6.0, 6.0)
    return entries * scale_grid(second, row_total, HEADS * HD)


def draw_video_key(key, part):
    key = jax.random.fold_in(key, 1)
    entries = base_entries(key, TOKENS)
    return entries.astype(jnp.bfloat16)


def draw_video_query(key, part):
    key = jax.random.fold_in(key, 2)
    first = jax.random.fold_in(key, 0)
    entries = base_entries(first, TOKENS)
    return entries.astype(jnp.bfloat16)


def draw_text_key(key, part):
    key = jax.random.fold_in(key, 3)
    entries = base_entries(key, TEXT)
    return entries.astype(jnp.bfloat16)


def draw_cross_query(key, part):
    key = jax.random.fold_in(key, 4)
    first = jax.random.fold_in(key, 0)
    entries = base_entries(first, TOKENS)
    return entries.astype(jnp.bfloat16)


def draw_text_mask(key, part):
    key = jax.random.fold_in(key, 5)
    length = jax.random.randint(key, (), TEXT // 8, TEXT + 1)
    return (jnp.arange(TEXT) < length).astype(jnp.int32)


def block_levels(rng, shape, cuts, least, largest):
    def one(axis_at, blocks):
        heights = jax.random.uniform(jax.random.fold_in(jax.random.fold_in(rng, 6), axis_at), (blocks,), jnp.float32, least / len(cuts), largest / len(cuts))
        return jnp.repeat(jnp.exp(heights), shape[axis_at] // blocks).reshape((-1,) + (1,) * (len(shape) - axis_at - 1))

    level = one(*cuts[0])
    for cut in cuts[1:]:
        level = level * one(*cut)
    return level


def noise(stream_key, shape, deviation, reach, shards=(), kind=jnp.bfloat16):
    drawn = deviation * jax.random.normal(stream_key, shape, jnp.float32)
    if shards:
        drawn = drawn * block_levels(stream_key, shape, shards, -0.22, 0.18)
    return jnp.clip(drawn, -reach, reach).astype(kind)


def setup_inputs(seed: int = 0) -> dict:
    arg_keys = jax.random.split(jax.random.key(seed), 11)
    video_query = draw_video_query(jax.random.fold_in(arg_keys[10], 71), 0)
    video_key = draw_video_key(jax.random.fold_in(arg_keys[10], 71), 0)
    video_value = noise(arg_keys[2], (TOKENS, HEADS * HD), 1.0, 6.0, ((0, 64), (1, 4)))
    cross_query = draw_cross_query(jax.random.fold_in(arg_keys[10], 71), 0)
    text_key = draw_text_key(jax.random.fold_in(arg_keys[10], 71), 0)
    text_value = noise(arg_keys[5], (TEXT, HEADS * HD), 1.0, 6.0, ((0, 64), (1, 4)))
    text_mask = draw_text_mask(jax.random.fold_in(arg_keys[10], 71), 0)
    norm_gains = jnp.clip(jnp.exp(math.log(2.5) - 1.13943427 * jax.random.uniform(arg_keys[7], (4, HEADS * HD), jnp.float32) ** block_levels(arg_keys[7], (4, HEADS * HD), ((1, 4),), -0.2, 0.2)), 0.8, 2.5)
    gate_table = noise(arg_keys[8], (STEPS, HEADS * HD), 1.0, 4.0, ((1, 4),), jnp.float32)
    timestep = jax.random.randint(arg_keys[9], (1,), 0, STEPS).astype(jnp.int32)
    return {"video_query": video_query, "video_key": video_key, "video_value": video_value, "cross_query": cross_query, "text_key": text_key, "text_value": text_value, "text_mask": text_mask, "norm_gains": norm_gains, "gate_table": gate_table, "timestep": timestep}


NEG_FILL = -1e+30

def normalize(matrix, gains_row):
    values = matrix.astype(jnp.float32)
    meansq = lax.optimization_barrier(jnp.mean(values * values, axis=1, keepdims=True))
    return (values * lax.rsqrt(meansq + 1e-06) * gains_row).astype(jnp.bfloat16)

def attend(queries, key_rows, value_rows, usable):
    row_count = queries.shape[0]
    key_count = key_rows.shape[0]
    query_heads = queries.reshape(row_count, HEADS, HD).transpose(1, 0, 2)
    key_heads = key_rows.reshape(key_count, HEADS, HD).transpose(1, 0, 2)
    value_heads = value_rows.reshape(key_count, HEADS, HD).transpose(1, 0, 2)

    def single(operands):
        query_part, key_part, value_part = operands
        scores = jnp.dot(query_part, key_part.T, preferred_element_type=jnp.float32) * HD ** (-0.5)
        scores = jnp.where(usable[None, :], scores, NEG_FILL)
        maxima = lax.optimization_barrier(jnp.max(scores, axis=1, keepdims=True))
        weights = jnp.where(usable[None, :], jnp.exp(scores - maxima), 0.0)
        totals = lax.optimization_barrier(jnp.sum(weights, axis=1, keepdims=True))
        summed = jnp.dot(weights.astype(jnp.bfloat16), value_part, preferred_element_type=jnp.float32)
        return summed / totals
    result = lax.map(single, (query_heads, key_heads, value_heads))
    return result.transpose(1, 0, 2).reshape(row_count, HEADS * HD)

def reference(video_query, video_key, video_value, cross_query, text_key, text_value, text_mask, norm_gains, gate_table, timestep):
    query_norm = normalize(video_query, norm_gains[0])
    key_norm = normalize(video_key, norm_gains[1])
    cross_norm = normalize(cross_query, norm_gains[2])
    text_norm = normalize(text_key, norm_gains[3])
    every_token = jnp.ones((video_key.shape[0],), dtype=bool)
    self_out = attend(query_norm, key_norm, video_value, every_token)
    cross_out = attend(cross_norm, text_norm, text_value, text_mask > 0)
    gating = lax.dynamic_slice_in_dim(gate_table, timestep[0].astype(jnp.int32), 1, 0)[0]
    return (gating * self_out + cross_out).astype(jnp.bfloat16)
```

```python
import jax
import jax.numpy as jnp
import numpy as np
from jax import lax
from jax.experimental import pallas as pl
from jax.experimental.pallas import tpu as pltpu
from jax.sharding import Mesh, PartitionSpec as P

HEADS = 20
HD = 128
LOG2E = 1.4426950408889634
SCALE2 = HD ** (-0.5) * LOG2E
PAD_MARK = 1e30
PAD_TEST = 1e20
NEG_FILL = -1e30
ROWS = 128
COLS = 640
HPD = 5
GROUP = 8
TEXT_ROWS = 16
OUT_ROWS = COLS + 16 + COLS


def squares(matrix):
    values = matrix.astype(jnp.float32)
    return jnp.sum(values * values, axis=1)


def rescale(matrix, totals, gains_row):
    values = matrix.astype(jnp.float32)
    factor = lax.rsqrt(totals / (HEADS * HD) + 1e-06)
    return (values * factor[:, None] * gains_row).astype(jnp.bfloat16)


def shift(array, step):
    return lax.ppermute(array, "z", [(i, (i + step) % 8) for i in range(8)])


def spread(array, dy, dx):
    pairs = []
    for y in range(4):
        for x in range(2):
            pairs.append((y * 2 + x, ((y + dy) % 4) * 2 + (x + dx) % 2))
    return lax.ppermute(array, ("y", "xh"), pairs)


def dot(a, b, ca, cb):
    return lax.dot_general(a, b, (((ca,), (cb,)), ((), ())), preferred_element_type=jnp.float32)


def flash_kernel(slot_ref, *refs):
    q_refs = refs[:8]
    c_refs = refs[8:15]
    k4_ref, v4_ref = refs[15:17]
    out_ref = refs[17]
    k_s, vt_s, tk_s, tv_s = refs[18:]
    for h in range(HPD):
        cols = slice(h * HD, (h + 1) * HD)
        for n, ref in enumerate(c_refs):
            k_s[n * ROWS:(n + 1) * ROWS, :] = ref[0:ROWS, cols]
            vt_s[:, n * ROWS:(n + 1) * ROWS] = ref[ROWS:2 * ROWS, cols].T
            text = ref[2 * ROWS:2 * ROWS + TEXT_ROWS, cols].astype(jnp.float32)
            tk_s[n * 8:(n + 1) * 8, :] = text[0:8]
            tv_s[n * 8:(n + 1) * 8, :] = text[8:16]
        k_s[7 * ROWS:8 * ROWS, :] = k4_ref[:, cols]
        vt_s[:, 7 * ROWS:8 * ROWS] = v4_ref[0:ROWS, cols].T
        text = v4_ref[ROWS:ROWS + TEXT_ROWS, cols].astype(jnp.float32)
        tk_s[56:64, :] = text[0:8]
        tv_s[56:64, :] = text[8:16]
        text_k = tk_s[...].astype(jnp.bfloat16)
        text_v = tv_s[...].astype(jnp.bfloat16)
        for pair in range(4):
            q = jnp.concatenate([q_refs[2 * pair][:, cols], q_refs[2 * pair + 1][:, cols]], axis=0)
            s = dot(k_s[...], q, 1, 1)
            top = jnp.max(s, axis=0, keepdims=True)
            p = jnp.exp2((s - top) * SCALE2)
            total = jnp.sum(p, axis=0, keepdims=True)
            o = dot(vt_s[...], p.astype(jnp.bfloat16), 1, 0)
            o = (o * (1.0 / total)).astype(jnp.bfloat16)
            level = top * SCALE2 + jnp.log2(total)
            hi = level.astype(jnp.bfloat16).astype(jnp.float32)
            rest = level - hi
            mid = rest.astype(jnp.bfloat16).astype(jnp.float32)
            low = rest - mid
            for half in range(2):
                slot = slot_ref[2 * pair + half]
                lanes = slice(half * ROWS, (half + 1) * ROWS)
                out_ref[slot, h * HD:(h + 1) * HD, :] = o[:, lanes]
                stats = jnp.concatenate([hi[:, lanes], mid[:, lanes], low[:, lanes]], axis=0)
                if h == 0:
                    out_ref[slot, COLS:COLS + 16, :] = jnp.zeros((16, ROWS), jnp.bfloat16)
                out_ref[slot, COLS + 3 * h:COLS + 3 * h + 3, :] = stats.astype(jnp.bfloat16)
                base = COLS + 16 + h * HD
                out_ref[slot, base:base + 64, :] = text_k
                out_ref[slot, base + 64:base + 128, :] = text_v


def final_kernel(in_ref, qc_ref, gate_ref, out_ref):
    for h in range(HPD):
        cols = slice(h * HD, (h + 1) * HD)
        levels = []
        for j in range(GROUP):
            stats = in_ref[j, COLS:COLS + 16, :].astype(jnp.float32)[3 * h:3 * h + 3]
            levels.append(stats[0:1] + stats[1:2] + stats[2:3])
        top = levels[0]
        for level in levels[1:]:
            top = jnp.maximum(top, level)
        shares = [jnp.exp2(level - top) for level in levels]
        total = shares[0]
        for share in shares[1:]:
            total = total + share
        inverse = 1.0 / total
        own = jnp.zeros((HD, ROWS), jnp.float32)
        for j in range(GROUP):
            own = own + in_ref[j, h * HD:(h + 1) * HD, :].astype(jnp.float32) * (shares[j] * inverse)
        base = COLS + 16 + h * HD
        keys = jnp.concatenate([in_ref[j, base:base + 64, :] for j in range(GROUP)], axis=0)
        values = jnp.concatenate([in_ref[j, base + 64:base + 128, :] for j in range(GROUP)], axis=0)
        s = dot(keys, qc_ref[:, cols], 1, 1)
        real = keys[:, 0:1].astype(jnp.float32) < PAD_TEST
        s = jnp.where(real, s, NEG_FILL)
        top = jnp.max(s, axis=0, keepdims=True)
        p = jnp.where(real, jnp.exp2((s - top) * SCALE2), 0.0)
        total = jnp.sum(p, axis=0, keepdims=True)
        cross = dot(values, p.astype(jnp.bfloat16), 0, 0) * (1.0 / total)
        out_ref[:, cols] = (gate_ref[:, cols] * own.T + cross.T).astype(jnp.bfloat16)


VM = pl.BlockSpec(memory_space=pltpu.VMEM)


def local(
    video_query,
    video_key,
    video_value,
    cross_query,
    text_key,
    text_value,
    text_mask,
    norm_gains,
    gate_table,
    timestep,
):
    norm_sums = lax.psum(
        jnp.concatenate([squares(video_query), squares(video_key), squares(cross_query), squares(text_key)]),
        "head",
    )
    key_norm = rescale(video_key, norm_sums[128:256], norm_gains[1])
    text_norm = rescale(text_key, norm_sums[384:392], norm_gains[3])
    text_norm = jnp.where(text_mask[:, None] > 0, text_norm, jnp.bfloat16(PAD_MARK))
    own = jnp.concatenate([key_norm, video_value, text_norm, text_value], axis=0)
    query_norm = rescale(video_query, norm_sums[0:128], norm_gains[0])
    cross_norm = rescale(cross_query, norm_sums[256:384], norm_gains[2])

    up1, down1 = shift(own, 1), shift(own, -1)
    up2, down2 = shift(up1, 1), shift(down1, -1)
    up3, down3 = shift(up2, 1), shift(down2, -1)
    key4 = shift(up3[:ROWS], 1)
    value4 = shift(down3[ROWS:], -1)

    moves = [(0, 0), (0, 1), (1, 0), (1, 1), (2, 0), (2, 1), (3, 0), (3, 1)]
    queries = [query_norm] + [spread(query_norm, dy, dx) for dy, dx in moves[1:]]
    y, x = lax.axis_index("y"), lax.axis_index("xh")
    slots = jnp.stack([((y - dy) % 4) * 2 + (x - dx) % 2 for dy, dx in moves]).astype(jnp.int32)

    partial = pl.pallas_call(
        flash_kernel,
        out_shape=jax.ShapeDtypeStruct((GROUP, OUT_ROWS, ROWS), jnp.bfloat16),
        in_specs=[pl.BlockSpec(memory_space=pltpu.SMEM)] + [VM] * 17,
        out_specs=VM,
        scratch_shapes=[
            pltpu.VMEM((1024, HD), jnp.bfloat16),
            pltpu.VMEM((HD, 1024), jnp.bfloat16),
            pltpu.VMEM((64, HD), jnp.float32),
            pltpu.VMEM((64, HD), jnp.float32),
        ],
        compiler_params=pltpu.CompilerParams(vmem_limit_bytes=48 * 1024 * 1024),
        cost_estimate=pl.CostEstimate(flops=2700000000, bytes_accessed=8000000, transcendentals=5242880),
    )(slots, *queries, own, up1, up2, up3, down1, down2, down3, key4, value4)

    received = lax.all_to_all(partial, ("y", "xh"), 0, 0)
    gating = lax.dynamic_slice_in_dim(gate_table, timestep[0], 1, 0)
    return pl.pallas_call(
        final_kernel,
        out_shape=jax.ShapeDtypeStruct((ROWS, COLS), jnp.bfloat16),
        in_specs=[VM] * 3,
        out_specs=VM,
        compiler_params=pltpu.CompilerParams(vmem_limit_bytes=32 * 1024 * 1024),
    )(received, cross_norm, gating)


def solution(mesh):
    grid = Mesh(mesh.devices.reshape(4, 2, 8, 4), ("y", "xh", "z", "head"))
    tokens = ("y", "xh", "z")
    placed = (
        P(tokens, "head"),
        P(tokens, "head"),
        P(tokens, "head"),
        P(tokens, "head"),
        P(tokens, "head"),
        P(tokens, "head"),
        P(tokens),
        P(None, "head"),
        P(None, "head"),
        P(),
    )
    return jax.shard_map(
        local, mesh=grid, in_specs=placed, out_specs=P(tokens, "head"), check_vma=False
    )
```

```python
import jax
import jax.numpy as jnp
from jax import lax
from jax.experimental import pallas as pl
from jax.experimental.pallas import tpu as pltpu
from jax.sharding import Mesh, PartitionSpec as P

HEADS = 20
HD = 128
LOG2E = 1.4426950408889634
SCALE2 = HD ** (-0.5) * LOG2E
PAD_MARK = 1e30
PAD_TEST = 1e20
NEG_FILL = -1e30
ROWS = 128
COLS = 640
HPD = 5
GROUP = 8
OUT_ROWS = COLS + 16
MIB = 1024 * 1024

SM = pl.BlockSpec(memory_space=pltpu.SMEM)


def dot(a, b, ca, cb):
    return lax.dot_general(a, b, (((ca,), (cb,)), ((), ())), preferred_element_type=jnp.float32)


def thirds(value):
    hi = value.astype(jnp.bfloat16).astype(jnp.float32)
    rest = value - hi
    mid = rest.astype(jnp.bfloat16).astype(jnp.float32)
    return hi, mid, rest - mid


def columns_of(row):
    return jnp.broadcast_to(row, (ROWS, ROWS)).T


def factor_of(row):
    return lax.rsqrt(columns_of(row) * (1.0 / (HEADS * HD)) + 1e-06)


def sums_kernel(q_ref, k_ref, c_ref, t_ref, out_ref):
    lane = lax.broadcasted_iota(jnp.int32, (ROWS, ROWS), 1)
    table = jnp.zeros((ROWS, ROWS), jnp.float32)
    for n, ref in enumerate((q_ref, k_ref, c_ref)):
        values = ref[...].astype(jnp.float32)
        table = jnp.where(lane == n, jnp.sum(values * values, axis=1, keepdims=True), table)
    table = table.T
    values = t_ref[...].astype(jnp.float32)
    text = jnp.sum(values * values, axis=1, keepdims=True)
    text = jnp.where(lax.broadcasted_iota(jnp.int32, (8, ROWS), 1) == 0, text, 0.0)
    text = jnp.concatenate([text, jnp.zeros((ROWS - 8, ROWS), jnp.float32)], axis=0).T
    row = lax.broadcasted_iota(jnp.int32, (8, ROWS), 0)
    out_ref[...] = jnp.where(row == 3, text[0:1], table[0:8])


def key_kernel(mask_ref, k_ref, v_ref, tk_ref, tv_ref, part_ref, other_ref, gains_ref, out_ref):
    sums = part_ref[...] + other_ref[...]
    k_factor = factor_of(sums[1:2])
    t_factor = factor_of(sums[3:4])[0:8]
    row = lax.broadcasted_iota(jnp.int32, (8, ROWS), 0)
    usable = jnp.zeros((8, ROWS), jnp.int32)
    for n in range(8):
        usable = jnp.where(row == n, mask_ref[n], usable)
    for h in range(HPD):
        cols = slice(h * HD, (h + 1) * HD)
        k = k_ref[:, cols].astype(jnp.float32) * k_factor * gains_ref[1:2, cols]
        out_ref[0:ROWS, cols] = k.astype(jnp.bfloat16)
        t = tk_ref[:, cols].astype(jnp.float32) * t_factor * gains_ref[3:4, cols]
        t = jnp.where(usable > 0, t, PAD_MARK)
        text = jnp.concatenate([t, tv_ref[:, cols].astype(jnp.float32)], axis=0)
        out_ref[2 * ROWS:2 * ROWS + 16, cols] = text.astype(jnp.bfloat16)
    out_ref[ROWS:2 * ROWS, :] = v_ref[...]


def query_kernel(q_ref, c_ref, part_ref, other_ref, gains_ref, q_out, c_out):
    sums = part_ref[...] + other_ref[...]
    q_factor = factor_of(sums[0:1])
    c_factor = factor_of(sums[2:3])
    for h in range(HPD):
        cols = slice(h * HD, (h + 1) * HD)
        q = (q_ref[:, cols].astype(jnp.float32) * q_factor * gains_ref[0:1, cols]).astype(jnp.bfloat16)
        for j in range(GROUP):
            q_out[j, :, cols] = q
        c_out[:, cols] = (c_ref[:, cols].astype(jnp.float32) * c_factor * gains_ref[2:3, cols]).astype(jnp.bfloat16)


def text_kernel(*refs):
    parts = [ref[...].astype(jnp.float32) for ref in refs[:8]]
    out_ref = refs[8]
    keys = jnp.concatenate([part[0:8] for part in parts], axis=0).astype(jnp.bfloat16)
    values = jnp.concatenate([part[8:16] for part in parts], axis=0).astype(jnp.bfloat16)
    for j in range(GROUP):
        out_ref[j, 0:64, :] = keys
        out_ref[j, 64:128, :] = values


def flash_kernel(q_ref, *refs):
    c_refs = refs[:7]
    k4_ref, v4_ref = refs[7:9]
    out_ref = refs[9]
    vt_s, s_s, p_s, stat_s = refs[10:]
    stat_s[...] = jnp.zeros_like(stat_s)
    stat_row = lax.broadcasted_iota(jnp.int32, (16, ROWS), 0)

    def head(h, carry):
        cols = pl.ds(pl.multiple_of(h * HD, HD), HD)
        for n in range(8):
            value = c_refs[n][ROWS:2 * ROWS, cols] if n < 7 else v4_ref[:, cols]
            vt_s[:, n * ROWS:(n + 1) * ROWS] = value.T
        for pair in range(4):
            q = jnp.concatenate([q_ref[2 * pair, :, cols], q_ref[2 * pair + 1, :, cols]], axis=0)
            top = None
            for n in range(8):
                key = c_refs[n][0:ROWS, cols] if n < 7 else k4_ref[:, cols]
                s = dot(key, q, 1, 1)
                s_s[pair % 2, n * ROWS:(n + 1) * ROWS, :] = s
                part = jnp.max(s.reshape(16, 8, 256), axis=0)
                top = part if top is None else jnp.maximum(top, part)
            top = jnp.max(top, axis=0, keepdims=True)
            total = jnp.zeros((8, 256), jnp.float32)
            for n in range(8):
                p = jnp.exp2((s_s[pair % 2, n * ROWS:(n + 1) * ROWS, :] - top) * SCALE2)
                total = total + jnp.sum(p.reshape(16, 8, 256), axis=0)
                p_s[pair % 2, n * ROWS:(n + 1) * ROWS, :] = p.astype(jnp.bfloat16)
            total = jnp.sum(total, axis=0, keepdims=True)
            o = dot(vt_s[...], p_s[pair % 2], 1, 0)
            o = (o * (1.0 / total)).astype(jnp.bfloat16)
            hi, mid, low = thirds(top * SCALE2 + jnp.log2(total))
            for half in range(2):
                slot = 2 * pair + half
                lanes = slice(half * ROWS, (half + 1) * ROWS)
                out_ref[slot, pl.ds(pl.multiple_of(h * HD, HD), HD), :] = o[:, lanes]
                stats = jnp.where(stat_row == 3 * h, hi[:, lanes], stat_s[slot])
                stats = jnp.where(stat_row == 3 * h + 1, mid[:, lanes], stats)
                stat_s[slot] = jnp.where(stat_row == 3 * h + 2, low[:, lanes], stats)
        return carry

    lax.fori_loop(0, HPD, head, 0)
    for slot in range(GROUP):
        out_ref[slot, COLS:OUT_ROWS, :] = stat_s[slot].astype(jnp.bfloat16)


def cross_kernel(text_ref, qc_ref, out_ref):
    for h in range(HPD):
        cols = slice(h * HD, (h + 1) * HD)
        keys = jnp.concatenate([text_ref[j, 0:64, cols] for j in range(GROUP)], axis=0)
        values = jnp.concatenate([text_ref[j, 64:128, cols] for j in range(GROUP)], axis=0)
        s = dot(keys, qc_ref[:, cols], 1, 1)
        real = keys[:, 0:1].astype(jnp.float32) < PAD_TEST
        s = jnp.where(real, s, NEG_FILL)
        top = jnp.max(s, axis=0, keepdims=True)
        p = jnp.where(real, jnp.exp2((s - top) * SCALE2), 0.0)
        total = jnp.sum(p, axis=0, keepdims=True)
        cross = dot(values, p.astype(jnp.bfloat16), 0, 0) * (1.0 / total)
        out_ref[:, cols] = cross.T


def final_kernel(in_ref, cross_ref, gate_ref, out_ref):
    for h in range(HPD):
        cols = slice(h * HD, (h + 1) * HD)
        levels = []
        for j in range(GROUP):
            stats = in_ref[j, COLS:OUT_ROWS, :].astype(jnp.float32)
            levels.append(stats[3 * h:3 * h + 1] + stats[3 * h + 1:3 * h + 2] + stats[3 * h + 2:3 * h + 3])
        top = levels[0]
        for level in levels[1:]:
            top = jnp.maximum(top, level)
        shares = [jnp.exp2(level - top) for level in levels]
        total = shares[0]
        for share in shares[1:]:
            total = total + share
        inverse = 1.0 / total
        own = jnp.zeros((HD, ROWS), jnp.float32)
        for j in range(GROUP):
            own = own + in_ref[j, h * HD:(h + 1) * HD, :].astype(jnp.float32) * (shares[j] * inverse)
        out_ref[:, cols] = (gate_ref[:, cols] * own.T + cross_ref[:, cols]).astype(jnp.bfloat16)


def block(shape, index=None):
    place = (0,) * len(shape) if index is None else index
    return pl.BlockSpec(shape, lambda i: place, pipeline_mode=pl.Buffered(buffer_count=1))


def call(kernel, shapes, arrays, specs=None, scratch=(), cost=None):
    return pl.pallas_call(
        kernel,
        grid=(1,),
        out_shape=[jax.ShapeDtypeStruct(shape, dtype) for shape, dtype in shapes],
        in_specs=specs or [block(array.shape) for array in arrays],
        out_specs=[block(shape) for shape, _ in shapes],
        scratch_shapes=list(scratch),
        compiler_params=pltpu.CompilerParams(vmem_limit_bytes=60 * MIB),
        cost_estimate=cost,
    )(*arrays)


def pass_kernel(*refs):
    pass


def gate(arrays, after=(), micros=10):
    arrays, after = list(arrays), list(after)
    return pl.pallas_call(
        pass_kernel,
        out_shape=[jax.ShapeDtypeStruct(array.shape, array.dtype) for array in arrays],
        in_specs=[pl.BlockSpec(memory_space=pl.ANY)] * (len(arrays) + len(after)),
        out_specs=[pl.BlockSpec(memory_space=pl.ANY)] * len(arrays),
        input_output_aliases={n: n for n in range(len(arrays))},
        compiler_params=pltpu.CompilerParams(vmem_limit_bytes=MIB),
        cost_estimate=pl.CostEstimate(flops=micros * 1150000000, bytes_accessed=1000, transcendentals=0),
    )(*arrays, *after)


def shift(array, step):
    return lax.ppermute(array, "z", [(i, (i + step) % 8) for i in range(8)])


def local(
    video_query,
    video_key,
    video_value,
    cross_query,
    text_key,
    text_value,
    text_mask,
    norm_gains,
    gate_table,
    timestep,
):
    bf16, f32 = jnp.bfloat16, jnp.float32
    (sums,) = call(sums_kernel, [((8, ROWS), f32)], [video_query, video_key, cross_query, text_key])
    part = sums + lax.ppermute(sums, "head", [(0, 1), (1, 0), (2, 3), (3, 2)])
    other = lax.ppermute(part, "head", [(0, 2), (2, 0), (1, 3), (3, 1)])
    arrays = [text_mask, video_key, video_value, text_key, text_value, part, other, norm_gains]
    (own,) = call(
        key_kernel,
        [((2 * ROWS + 16, COLS), bf16)],
        arrays,
        [SM] + [block(array.shape) for array in arrays[1:]],
    )
    up1, down1 = gate([shift(own, 1), shift(own, -1)])
    queries, cross_norm = call(
        query_kernel,
        [((GROUP, ROWS, COLS), bf16), ((ROWS, COLS), bf16)],
        [video_query, cross_query, part, other, norm_gains],
    )
    queries = lax.all_to_all(queries, ("y", "xh"), 0, 0)
    up2, down2 = gate([shift(up1, 1), shift(down1, -1)], micros=2)
    up3, down3 = gate([shift(up2, 1), shift(down2, -1)], after=[queries], micros=2)
    key4 = shift(up3[:ROWS], 1)
    value4 = shift(down3[ROWS:], -1)
    key4, value4 = gate([key4, value4])

    ring = [own, up1, up2, up3, down1, down2, down3]
    (text_part,) = call(
        text_kernel,
        [((GROUP, ROWS, COLS), bf16)],
        ring + [value4],
        [block((16, COLS), (16, 0))] * 7 + [block((16, COLS), (8, 0))],
    )
    text_whole = lax.all_to_all(text_part, ("y", "xh"), 0, 0)

    (partial,) = call(
        flash_kernel,
        [((GROUP, OUT_ROWS, ROWS), bf16)],
        [queries] + ring + [key4, value4],
        [block(queries.shape)] + [block((2 * ROWS, COLS))] * 7 + [block((ROWS, COLS))] * 2,
        [
            pltpu.VMEM((HD, 1024), bf16),
            pltpu.VMEM((2, 1024, 256), f32),
            pltpu.VMEM((2, 1024, 256), bf16),
            pltpu.VMEM((GROUP, 16, ROWS), f32),
        ],
        pl.CostEstimate(flops=15000000000, bytes_accessed=8000000, transcendentals=5242880),
    )

    received = lax.all_to_all(partial, ("y", "xh"), 0, 0)
    gating = lax.dynamic_slice_in_dim(gate_table, timestep[0], 1, 0)
    (cross,) = call(cross_kernel, [((ROWS, COLS), f32)], [text_whole, cross_norm])
    (out,) = call(final_kernel, [((ROWS, COLS), bf16)], [received, cross, gating])
    return out


def solution(mesh):
    grid = Mesh(mesh.devices.reshape(4, 2, 8, 4), ("y", "xh", "z", "head"))
    tokens = ("y", "xh", "z")
    placed = (
        P(tokens, "head"),
        P(tokens, "head"),
        P(tokens, "head"),
        P(tokens, "head"),
        P(tokens, "head"),
        P(tokens, "head"),
        P(tokens),
        P(None, "head"),
        P(None, "head"),
        P(),
    )
    return jax.shard_map(
        local, mesh=grid, in_specs=placed, out_specs=P(tokens, "head"), check_vma=False
    )
```

```python
import jax
import jax.numpy as jnp
from jax import lax
from jax.experimental import pallas as pl
from jax.experimental.pallas import tpu as pltpu
from jax.sharding import Mesh, PartitionSpec as P

HEADS = 20
HD = 128
LOG2E = 1.4426950408889634
SCALE2 = HD ** (-0.5) * LOG2E
PAD_MARK = 1e30
PAD_TEST = 1e20
NEG_FILL = -1e30
ROWS = 128
COLS = 640
HPD = 5
GROUP = 8
OUT_ROWS = COLS + 16
MIB = 1024 * 1024
SPAN = 256
PIECE = 32
PARTS = 1024 // SPAN
UNITS = HPD * PARTS

SM = pl.BlockSpec(memory_space=pltpu.SMEM)


def dot(a, b, ca, cb):
    return lax.dot_general(a, b, (((ca,), (cb,)), ((), ())), preferred_element_type=jnp.float32)


def thirds(value):
    hi = value.astype(jnp.bfloat16).astype(jnp.float32)
    rest = value - hi
    mid = rest.astype(jnp.bfloat16).astype(jnp.float32)
    return hi, mid, rest - mid


def columns_of(row):
    return jnp.broadcast_to(row, (ROWS, ROWS)).T


def factor_of(row):
    return lax.rsqrt(columns_of(row) * (1.0 / (HEADS * HD)) + 1e-06)


def sums_kernel(q_ref, k_ref, c_ref, t_ref, out_ref):
    lane = lax.broadcasted_iota(jnp.int32, (ROWS, ROWS), 1)
    table = jnp.zeros((ROWS, ROWS), jnp.float32)
    for n, ref in enumerate((q_ref, k_ref, c_ref)):
        values = ref[...].astype(jnp.float32)
        table = jnp.where(lane == n, jnp.sum(values * values, axis=1, keepdims=True), table)
    table = table.T
    values = t_ref[...].astype(jnp.float32)
    text = jnp.sum(values * values, axis=1, keepdims=True)
    text = jnp.where(lax.broadcasted_iota(jnp.int32, (8, ROWS), 1) == 0, text, 0.0)
    text = jnp.concatenate([text, jnp.zeros((ROWS - 8, ROWS), jnp.float32)], axis=0).T
    row = lax.broadcasted_iota(jnp.int32, (8, ROWS), 0)
    out_ref[...] = jnp.where(row == 3, text[0:1], table[0:8])


def key_kernel(mask_ref, k_ref, v_ref, tk_ref, tv_ref, part_ref, other_ref, gains_ref, out_ref, text_out):
    k_factor = factor_of(part_ref[1:2] + other_ref[1:2])
    t_factor = factor_of(part_ref[3:4] + other_ref[3:4])[0:8]
    row = lax.broadcasted_iota(jnp.int32, (8, ROWS), 0)
    usable = jnp.zeros((8, ROWS), jnp.int32)
    for n in range(8):
        usable = jnp.where(row == n, mask_ref[n], usable)
    for h in range(HPD):
        cols = slice(h * HD, (h + 1) * HD)
        k = k_ref[:, cols].astype(jnp.float32) * k_factor * gains_ref[1:2, cols]
        out_ref[0:ROWS, cols] = k.astype(jnp.bfloat16)
        t = tk_ref[:, cols].astype(jnp.float32) * t_factor * gains_ref[3:4, cols]
        t = jnp.where(usable > 0, t, PAD_MARK)
        text = jnp.concatenate([t, tv_ref[:, cols].astype(jnp.float32)], axis=0).astype(jnp.bfloat16)
        out_ref[2 * ROWS:2 * ROWS + 16, cols] = text
        text_out[:, cols] = text
    out_ref[ROWS:2 * ROWS, :] = v_ref[...]


def query_kernel(q_ref, part_ref, other_ref, gains_ref, out_ref):
    factor = factor_of(part_ref[0:1] + other_ref[0:1])
    for h in range(HPD):
        cols = slice(h * HD, (h + 1) * HD)
        q = (q_ref[:, cols].astype(jnp.float32) * factor * gains_ref[0:1, cols]).astype(jnp.bfloat16)
        for j in range(GROUP):
            out_ref[j, :, cols] = q


def text_kernel(*refs):
    parts = [ref[...].astype(jnp.float32) for ref in refs[:8]]
    out_ref = refs[8]
    keys = jnp.concatenate([part[0:8] for part in parts], axis=0).astype(jnp.bfloat16)
    values = jnp.concatenate([part[8:16] for part in parts], axis=0).astype(jnp.bfloat16)
    for j in range(GROUP):
        out_ref[j, 0:64, :] = keys
        out_ref[j, 64:128, :] = values


def unit_place(unit):
    unit = jnp.clip(unit, 0, UNITS - 1)
    head = lax.div(unit, PARTS)
    first = lax.rem(unit, PARTS) * (SPAN // ROWS)
    return head, first, pl.ds(pl.multiple_of(head * HD, HD), HD)


def flash_kernel(q_ref, *refs):
    c_refs = refs[:8]
    out_ref = refs[8]
    k_s, v_s, s_a, s_b, p_a, p_b, i_a, i_b, stat_s = refs[9:]
    lane = lax.broadcasted_iota(jnp.int32, (PIECE, ROWS), 1)
    stat_s[...] = jnp.zeros_like(stat_s)
    for n in range(8):
        rows = slice(n * ROWS, (n + 1) * ROWS)
        k_s[rows, :] = c_refs[n][0:ROWS, :]
        v_s[rows, :] = c_refs[n][ROWS:2 * ROWS, :]

    def score(unit, s_ref, tile):
        _, first, cols = unit_place(unit)
        q = q_ref[pl.ds(first, SPAN // ROWS), :, cols].reshape(SPAN, HD)
        keys = slice(tile * 256, (tile + 1) * 256)
        s_ref[:, keys] = dot(q, k_s[keys, cols], 1, 1)

    def soften(unit, s_ref, p_ref, i_ref, piece):
        head, first, _ = unit_place(unit)
        rows = slice(piece * PIECE, (piece + 1) * PIECE)
        s = s_ref[rows, :]
        top = s[:, 0:ROWS]
        for n in range(1, 8):
            top = jnp.maximum(top, s[:, n * ROWS:(n + 1) * ROWS])
        top = jnp.max(top, axis=1, keepdims=True)
        p = jnp.exp2((s - top) * SCALE2)
        total = p[:, 0:ROWS]
        for n in range(1, 8):
            total = total + p[:, n * ROWS:(n + 1) * ROWS]
        total = jnp.sum(total, axis=1, keepdims=True)
        p_ref[rows, :] = p.astype(jnp.bfloat16)
        i_ref[rows, :] = jnp.broadcast_to(1.0 / total, (PIECE, ROWS))
        hi, mid, low = thirds(jnp.broadcast_to(top * SCALE2 + jnp.log2(total), (PIECE, ROWS)))
        slot = first + piece * PIECE // ROWS
        inner = slice(piece * PIECE % ROWS, piece * PIECE % ROWS + PIECE)
        stats = jnp.where(lane == 3 * head, hi, stat_s[slot, inner, :])
        stats = jnp.where(lane == 3 * head + 1, mid, stats)
        stat_s[slot, inner, :] = jnp.where(lane == 3 * head + 2, low, stats)

    def blend(unit, p_ref, i_ref):
        head, first, cols = unit_place(unit)
        o = (dot(p_ref[...], v_s[:, cols], 1, 0) * i_ref[...]).astype(jnp.bfloat16)
        for n in range(SPAN // ROWS):
            out_ref[first + n, pl.ds(pl.multiple_of(head * HD, HD), HD), :] = o[n * ROWS:(n + 1) * ROWS]

    def phase(unit, s_next, s_now, p_now, i_now, p_last, i_last):
        blend(unit - 1, p_last, i_last)
        pieces = SPAN // PIECE
        for piece in range(pieces):
            if piece % (pieces // 4) == 0:
                score(unit + 1, s_next, piece // (pieces // 4))
            soften(unit, s_now, p_now, i_now, piece)

    for tile in range(4):
        score(0, s_a, tile)

    def step(i, carry):
        phase(2 * i, s_b, s_a, p_a, i_a, p_b, i_b)
        phase(2 * i + 1, s_a, s_b, p_b, i_b, p_a, i_a)
        return carry

    lax.fori_loop(0, UNITS // 2, step, 0)
    blend(UNITS - 1, p_b, i_b)
    for slot in range(GROUP):
        out_ref[slot, COLS:OUT_ROWS, :] = stat_s[slot].T[0:16].astype(jnp.bfloat16)


def cross_kernel(text_ref, c_ref, part_ref, other_ref, gains_ref, out_ref):
    factor = factor_of(part_ref[2:3] + other_ref[2:3])
    for h in range(HPD):
        cols = slice(h * HD, (h + 1) * HD)
        queries = (c_ref[:, cols].astype(jnp.float32) * factor * gains_ref[2:3, cols]).astype(jnp.bfloat16)
        keys = jnp.concatenate([text_ref[j, 0:64, cols] for j in range(GROUP)], axis=0)
        values = jnp.concatenate([text_ref[j, 64:128, cols] for j in range(GROUP)], axis=0)
        s = dot(keys, queries, 1, 1)
        real = keys[:, 0:1].astype(jnp.float32) < PAD_TEST
        s = jnp.where(real, s, NEG_FILL)
        top = jnp.max(s, axis=0, keepdims=True)
        p = jnp.where(real, jnp.exp2((s - top) * SCALE2), 0.0)
        total = jnp.sum(p, axis=0, keepdims=True)
        cross = dot(values, p.astype(jnp.bfloat16), 0, 0) * (1.0 / total)
        out_ref[:, cols] = cross.T


def final_kernel(in_ref, cross_ref, gate_ref, out_ref):
    for h in range(HPD):
        cols = slice(h * HD, (h + 1) * HD)
        levels = []
        for j in range(GROUP):
            stats = in_ref[j, COLS:OUT_ROWS, :].astype(jnp.float32)
            levels.append(stats[3 * h:3 * h + 1] + stats[3 * h + 1:3 * h + 2] + stats[3 * h + 2:3 * h + 3])
        top = levels[0]
        for level in levels[1:]:
            top = jnp.maximum(top, level)
        shares = [jnp.exp2(level - top) for level in levels]
        total = shares[0]
        for share in shares[1:]:
            total = total + share
        inverse = 1.0 / total
        shares = jnp.concatenate([share * inverse for share in shares], axis=0)
        shares = jnp.concatenate([shares, jnp.zeros((ROWS - GROUP, ROWS), jnp.float32)], axis=0).T
        own = jnp.zeros((ROWS, HD), jnp.float32)
        for j in range(GROUP):
            own = own + in_ref[j, h * HD:(h + 1) * HD, :].astype(jnp.float32) * shares[:, j:j + 1]
        out_ref[:, cols] = (gate_ref[:, cols] * own + cross_ref[:, cols]).astype(jnp.bfloat16)


def block(shape, index=None):
    place = (0,) * len(shape) if index is None else index
    return pl.BlockSpec(shape, lambda i: place, pipeline_mode=pl.Buffered(buffer_count=1))


def call(kernel, shapes, arrays, specs=None, scratch=(), cost=None):
    return pl.pallas_call(
        kernel,
        grid=(1,),
        out_shape=[jax.ShapeDtypeStruct(shape, dtype) for shape, dtype in shapes],
        in_specs=specs or [block(array.shape) for array in arrays],
        out_specs=[block(shape) for shape, _ in shapes],
        scratch_shapes=list(scratch),
        compiler_params=pltpu.CompilerParams(vmem_limit_bytes=60 * MIB),
        cost_estimate=cost,
    )(*arrays)


def flash_call(queries, ring):
    bf16, f32 = jnp.bfloat16, jnp.float32
    return call(
        flash_kernel,
        [((GROUP, OUT_ROWS, ROWS), bf16)],
        [queries] + ring,
        [block((GROUP, ROWS, COLS))] + [block((2 * ROWS, COLS))] * 8,
        [
            pltpu.VMEM((1024, COLS), bf16),
            pltpu.VMEM((1024, COLS), bf16),
            pltpu.VMEM((SPAN, 1024), f32),
            pltpu.VMEM((SPAN, 1024), f32),
            pltpu.VMEM((SPAN, 1024), bf16),
            pltpu.VMEM((SPAN, 1024), bf16),
            pltpu.VMEM((SPAN, ROWS), f32),
            pltpu.VMEM((SPAN, ROWS), f32),
            pltpu.VMEM((GROUP, ROWS, ROWS), f32),
        ],
        pl.CostEstimate(flops=15000000000, bytes_accessed=8000000, transcendentals=5242880),
    )


def pass_kernel(*refs):
    pass


def gate(arrays, after=(), micros=10):
    arrays, after = list(arrays), list(after)
    return pl.pallas_call(
        pass_kernel,
        out_shape=[jax.ShapeDtypeStruct(array.shape, array.dtype) for array in arrays],
        in_specs=[pl.BlockSpec(memory_space=pl.ANY)] * (len(arrays) + len(after)),
        out_specs=[pl.BlockSpec(memory_space=pl.ANY)] * len(arrays),
        input_output_aliases={n: n for n in range(len(arrays))},
        compiler_params=pltpu.CompilerParams(vmem_limit_bytes=MIB),
        cost_estimate=pl.CostEstimate(flops=micros * 1150000000, bytes_accessed=1000, transcendentals=0),
    )(*arrays, *after)


def shift(array, step):
    return lax.ppermute(array, "z", [(i, (i + step) % 8) for i in range(8)])


def local(
    video_query,
    video_key,
    video_value,
    cross_query,
    text_key,
    text_value,
    text_mask,
    norm_gains,
    gate_table,
    timestep,
):
    bf16, f32 = jnp.bfloat16, jnp.float32
    (sums,) = call(sums_kernel, [((8, ROWS), f32)], [video_query, video_key, cross_query, text_key])
    part = sums + lax.ppermute(sums, "head", [(0, 1), (1, 0), (2, 3), (3, 2)])
    other = lax.ppermute(part, "head", [(0, 2), (2, 0), (1, 3), (3, 1)])
    arrays = [text_mask, video_key, video_value, text_key, text_value, part, other, norm_gains]
    own, text_own = call(
        key_kernel,
        [((2 * ROWS + 16, COLS), bf16), ((16, COLS), bf16)],
        arrays,
        [SM] + [block(array.shape) for array in arrays[1:]],
    )
    up1, down1 = gate([shift(own, 1), shift(own, -1)])
    (queries,) = call(
        query_kernel, [((GROUP, ROWS, COLS), bf16)], [video_query, part, other, norm_gains]
    )
    queries = lax.all_to_all(queries, ("y", "xh"), 0, 0)
    text4 = shift(text_own, 4)
    up2, down2 = gate([shift(up1, 1), shift(down1, -1)], after=[text4], micros=2)
    up3, down3 = gate([shift(up2, 1), shift(down2, -1)], after=[queries], micros=2)
    (far,) = gate([shift(up3, 1)])

    ring = [own, up1, up2, up3, down1, down2, down3]
    (text,) = call(
        text_kernel,
        [((GROUP, ROWS, COLS), bf16)],
        ring + [text4],
        [block((16, COLS), (16, 0))] * 7 + [block((16, COLS))],
    )
    text = lax.all_to_all(text, ("y", "xh"), 0, 0)

    (partial,) = flash_call(queries, ring + [far])

    received = lax.all_to_all(partial, ("y", "xh"), 0, 0)
    gating = lax.dynamic_slice_in_dim(gate_table, timestep[0], 1, 0)
    (cross,) = call(cross_kernel, [((ROWS, COLS), f32)], [text, cross_query, part, other, norm_gains])
    (out,) = call(final_kernel, [((ROWS, COLS), bf16)], [received, cross, gating])
    return out


def solution(mesh):
    grid = Mesh(mesh.devices.reshape(4, 2, 8, 4), ("y", "xh", "z", "head"))
    tokens = ("y", "xh", "z")
    placed = (
        P(tokens, "head"),
        P(tokens, "head"),
        P(tokens, "head"),
        P(tokens, "head"),
        P(tokens, "head"),
        P(tokens, "head"),
        P(tokens),
        P(None, "head"),
        P(None, "head"),
        P(),
    )
    return jax.shard_map(
        local, mesh=grid, in_specs=placed, out_specs=P(tokens, "head"), check_vma=False
    )
```

```python
import jax
import jax.numpy as jnp
from jax import lax
from jax.experimental import pallas as pl
from jax.experimental.pallas import tpu as pltpu
from jax.sharding import Mesh, PartitionSpec as P

HEADS = 20
HD = 128
LOG2E = 1.4426950408889634
SCALE2 = HD ** (-0.5) * LOG2E
PAD_MARK = 1e30
PAD_TEST = 1e20
NEG_FILL = -1e30
ROWS = 128
COLS = 640
HPD = 5
GROUP = 8
OUT_ROWS = COLS + 16
MIB = 1024 * 1024
LIMIT = 60
SPAN = 256
PIECE = 32
PARTS = 1024 // SPAN
UNITS = HPD * PARTS

VM = pl.BlockSpec(memory_space=pltpu.VMEM)


def dot(a, b, ca, cb):
    return lax.dot_general(a, b, (((ca,), (cb,)), ((), ())), preferred_element_type=jnp.float32)


def thirds(value):
    hi = value.astype(jnp.bfloat16).astype(jnp.float32)
    rest = value - hi
    mid = rest.astype(jnp.bfloat16).astype(jnp.float32)
    return hi, mid, rest - mid


def columns_of(row):
    return jnp.broadcast_to(row, (ROWS, ROWS)).T


def factor_of(row):
    return lax.rsqrt(columns_of(row) * (1.0 / (HEADS * HD)) + 1e-06)


def sums_kernel(q_ref, k_ref, c_ref, t_ref, out_ref):
    lane = lax.broadcasted_iota(jnp.int32, (ROWS, ROWS), 1)
    table = jnp.zeros((ROWS, ROWS), jnp.float32)
    for n, ref in enumerate((q_ref, k_ref, c_ref)):
        values = ref[...].astype(jnp.float32)
        table = jnp.where(lane == n, jnp.sum(values * values, axis=1, keepdims=True), table)
    table = table.T
    values = t_ref[...].astype(jnp.float32)
    text = jnp.sum(values * values, axis=1, keepdims=True)
    text = jnp.where(lax.broadcasted_iota(jnp.int32, (8, ROWS), 1) == 0, text, 0.0)
    text = jnp.concatenate([text, jnp.zeros((ROWS - 8, ROWS), jnp.float32)], axis=0).T
    row = lax.broadcasted_iota(jnp.int32, (8, ROWS), 0)
    out_ref[...] = jnp.where(row == 3, text[0:1], table[0:8])


def key_kernel(mask_ref, k_ref, v_ref, tk_ref, tv_ref, gains_ref, part_ref, other_ref, out_ref, text_out):
    k_factor = factor_of(part_ref[1:2] + other_ref[1:2])
    t_factor = factor_of(part_ref[3:4] + other_ref[3:4])[0:8]
    row = lax.broadcasted_iota(jnp.int32, (8, ROWS), 0)
    usable = jnp.zeros((8, ROWS), jnp.int32)
    for n in range(8):
        usable = jnp.where(row == n, mask_ref[n], usable)
    for h in range(HPD):
        cols = slice(h * HD, (h + 1) * HD)
        k = k_ref[:, cols].astype(jnp.float32) * k_factor * gains_ref[1:2, cols]
        out_ref[0:ROWS, cols] = k.astype(jnp.bfloat16)
        t = tk_ref[:, cols].astype(jnp.float32) * t_factor * gains_ref[3:4, cols]
        t = jnp.where(usable > 0, t, PAD_MARK)
        text = jnp.concatenate([t, tv_ref[:, cols].astype(jnp.float32)], axis=0).astype(jnp.bfloat16)
        out_ref[2 * ROWS:2 * ROWS + 16, cols] = text
        text_out[:, cols] = text
    out_ref[ROWS:2 * ROWS, :] = v_ref[...]


def query_kernel(q_ref, gains_ref, part_ref, other_ref, out_ref):
    factor = factor_of(part_ref[0:1] + other_ref[0:1])
    for h in range(HPD):
        cols = slice(h * HD, (h + 1) * HD)
        q = (q_ref[:, cols].astype(jnp.float32) * factor * gains_ref[0:1, cols]).astype(jnp.bfloat16)
        for j in range(GROUP):
            out_ref[j, :, cols] = q


def text_kernel(*refs):
    parts = [ref[...].astype(jnp.float32) for ref in refs[:8]]
    out_ref = refs[8]
    keys = jnp.concatenate([part[0:8] for part in parts], axis=0).astype(jnp.bfloat16)
    values = jnp.concatenate([part[8:16] for part in parts], axis=0).astype(jnp.bfloat16)
    for j in range(GROUP):
        out_ref[j, 0:64, :] = keys
        out_ref[j, 64:128, :] = values


def unit_place(unit):
    unit = jnp.clip(unit, 0, UNITS - 1)
    head = lax.div(unit, PARTS)
    first = lax.rem(unit, PARTS) * (SPAN // ROWS)
    return head, first, pl.ds(pl.multiple_of(head * HD, HD), HD)


def flash_kernel(q_ref, *refs):
    c_refs = refs[:8]
    out_ref = refs[8]
    k_s, v_s, s_a, s_b, p_a, p_b, i_a, i_b, stat_s = refs[9:]
    lane = lax.broadcasted_iota(jnp.int32, (PIECE, ROWS), 1)
    stat_s[...] = jnp.zeros_like(stat_s)
    for n in range(8):
        rows = slice(n * ROWS, (n + 1) * ROWS)
        k_s[rows, :] = c_refs[n][0:ROWS, :]
        v_s[rows, :] = c_refs[n][ROWS:2 * ROWS, :]

    def score(unit, s_ref, tile):
        _, first, cols = unit_place(unit)
        q = q_ref[pl.ds(first, SPAN // ROWS), :, cols].reshape(SPAN, HD)
        keys = slice(tile * 256, (tile + 1) * 256)
        s_ref[:, keys] = dot(q, k_s[keys, cols], 1, 1)

    def soften(unit, s_ref, p_ref, i_ref, piece):
        head, first, _ = unit_place(unit)
        rows = slice(piece * PIECE, (piece + 1) * PIECE)
        s = s_ref[rows, :]
        top = s[:, 0:ROWS]
        for n in range(1, 8):
            top = jnp.maximum(top, s[:, n * ROWS:(n + 1) * ROWS])
        top = jnp.max(top, axis=1, keepdims=True)
        p = jnp.exp2((s - top) * SCALE2)
        total = p[:, 0:ROWS]
        for n in range(1, 8):
            total = total + p[:, n * ROWS:(n + 1) * ROWS]
        total = jnp.sum(total, axis=1, keepdims=True)
        p_ref[rows, :] = p.astype(jnp.bfloat16)
        i_ref[rows, :] = jnp.broadcast_to(1.0 / total, (PIECE, ROWS))
        hi, mid, low = thirds(jnp.broadcast_to(top * SCALE2 + jnp.log2(total), (PIECE, ROWS)))
        slot = first + piece * PIECE // ROWS
        inner = slice(piece * PIECE % ROWS, piece * PIECE % ROWS + PIECE)
        stats = jnp.where(lane == 3 * head, hi, stat_s[slot, inner, :])
        stats = jnp.where(lane == 3 * head + 1, mid, stats)
        stat_s[slot, inner, :] = jnp.where(lane == 3 * head + 2, low, stats)

    def blend(unit, p_ref, i_ref):
        head, first, cols = unit_place(unit)
        o = (dot(p_ref[...], v_s[:, cols], 1, 0) * i_ref[...]).astype(jnp.bfloat16)
        for n in range(SPAN // ROWS):
            out_ref[first + n, pl.ds(pl.multiple_of(head * HD, HD), HD), :] = o[n * ROWS:(n + 1) * ROWS]

    def phase(unit, s_next, s_now, p_now, i_now, p_last, i_last):
        blend(unit - 1, p_last, i_last)
        pieces = SPAN // PIECE
        for piece in range(pieces):
            if piece % (pieces // 4) == 0:
                score(unit + 1, s_next, piece // (pieces // 4))
            soften(unit, s_now, p_now, i_now, piece)

    for tile in range(4):
        score(0, s_a, tile)

    def step(i, carry):
        phase(2 * i, s_b, s_a, p_a, i_a, p_b, i_b)
        phase(2 * i + 1, s_a, s_b, p_b, i_b, p_a, i_a)
        return carry

    lax.fori_loop(0, UNITS // 2, step, 0)
    blend(UNITS - 1, p_b, i_b)
    for slot in range(GROUP):
        out_ref[slot, COLS:OUT_ROWS, :] = stat_s[slot].T[0:16].astype(jnp.bfloat16)


def cross_kernel(text_ref, c_ref, gains_ref, part_ref, other_ref, out_ref):
    factor = factor_of(part_ref[2:3] + other_ref[2:3])
    for h in range(HPD):
        cols = slice(h * HD, (h + 1) * HD)
        queries = (c_ref[:, cols].astype(jnp.float32) * factor * gains_ref[2:3, cols]).astype(jnp.bfloat16)
        keys = jnp.concatenate([text_ref[j, 0:64, cols] for j in range(GROUP)], axis=0)
        values = jnp.concatenate([text_ref[j, 64:128, cols] for j in range(GROUP)], axis=0)
        s = dot(keys, queries, 1, 1)
        real = keys[:, 0:1].astype(jnp.float32) < PAD_TEST
        s = jnp.where(real, s, NEG_FILL)
        top = jnp.max(s, axis=0, keepdims=True)
        p = jnp.where(real, jnp.exp2((s - top) * SCALE2), 0.0)
        total = jnp.sum(p, axis=0, keepdims=True)
        cross = dot(values, p.astype(jnp.bfloat16), 0, 0) * (1.0 / total)
        out_ref[:, cols] = cross.T


def final_kernel(in_ref, cross_ref, gate_ref, out_ref):
    for h in range(HPD):
        cols = slice(h * HD, (h + 1) * HD)
        levels = []
        for j in range(GROUP):
            stats = in_ref[j, COLS:OUT_ROWS, :].astype(jnp.float32)
            levels.append(stats[3 * h:3 * h + 1] + stats[3 * h + 1:3 * h + 2] + stats[3 * h + 2:3 * h + 3])
        top = levels[0]
        for level in levels[1:]:
            top = jnp.maximum(top, level)
        shares = [jnp.exp2(level - top) for level in levels]
        total = shares[0]
        for share in shares[1:]:
            total = total + share
        inverse = 1.0 / total
        shares = jnp.concatenate([share * inverse for share in shares], axis=0)
        shares = jnp.concatenate([shares, jnp.zeros((ROWS - GROUP, ROWS), jnp.float32)], axis=0).T
        own = jnp.zeros((ROWS, HD), jnp.float32)
        for j in range(GROUP):
            own = own + in_ref[j, h * HD:(h + 1) * HD, :].astype(jnp.float32) * shares[:, j:j + 1]
        out_ref[:, cols] = (gate_ref[:, cols] * own + cross_ref[:, cols]).astype(jnp.bfloat16)


def in_hbm(array):
    return pltpu.with_memory_space_constraint(array, pltpu.HBM)


def in_vmem(array):
    return pltpu.with_memory_space_constraint(array, pltpu.VMEM)


def block(shape, index=None):
    place = (0,) * len(shape) if index is None else index
    return pl.BlockSpec(shape, lambda i: place, pipeline_mode=pl.Buffered(buffer_count=1))


def call(kernel, shapes, arrays, near=(), scalars=0, scratch=(), cost=None, free=()):
    ins, specs = [], []
    for n, array in enumerate(arrays):
        ins.append(array if n < scalars else in_hbm(array))
        specs.append(pl.BlockSpec(memory_space=pltpu.SMEM) if n < scalars else block(array.shape))
    for array in near:
        ins.append(in_vmem(array))
        specs.append(VM)
    for array, shape, index in free:
        ins.append(array)
        specs.append(block(shape, index))
    out_shape, out_specs = [], []
    for shape, dtype, place in shapes:
        out_shape.append(place(shape, dtype))
        out_specs.append(VM if place is pltpu.VMEM else block(shape))
    return pl.pallas_call(
        kernel,
        grid=(1,),
        out_shape=out_shape,
        in_specs=specs,
        out_specs=out_specs,
        scratch_shapes=list(scratch),
        compiler_params=pltpu.CompilerParams(vmem_limit_bytes=LIMIT * MIB),
        cost_estimate=cost,
    )(*ins)


def flash_call(queries, ring):
    bf16, f32 = jnp.bfloat16, jnp.float32
    return call(
        flash_kernel,
        [((GROUP, OUT_ROWS, ROWS), bf16, pltpu.HBM)],
        [queries],
        (),
        0,
        [
            pltpu.VMEM((1024, COLS), bf16),
            pltpu.VMEM((1024, COLS), bf16),
            pltpu.VMEM((SPAN, 1024), f32),
            pltpu.VMEM((SPAN, 1024), f32),
            pltpu.VMEM((SPAN, 1024), bf16),
            pltpu.VMEM((SPAN, 1024), bf16),
            pltpu.VMEM((SPAN, ROWS), f32),
            pltpu.VMEM((SPAN, ROWS), f32),
            pltpu.VMEM((GROUP, ROWS, ROWS), f32),
        ],
        pl.CostEstimate(flops=15000000000, bytes_accessed=8000000, transcendentals=5242880),
        [(array, (2 * ROWS, COLS), (0, 0)) for array in ring],
    )


def pass_kernel(*refs):
    pass


def gate(arrays, after=(), micros=10):
    arrays, after = list(arrays), list(after)
    return pl.pallas_call(
        pass_kernel,
        out_shape=[jax.ShapeDtypeStruct(array.shape, array.dtype) for array in arrays],
        in_specs=[pl.BlockSpec(memory_space=pl.ANY)] * (len(arrays) + len(after)),
        out_specs=[pl.BlockSpec(memory_space=pl.ANY)] * len(arrays),
        input_output_aliases={n: n for n in range(len(arrays))},
        compiler_params=pltpu.CompilerParams(vmem_limit_bytes=MIB),
        cost_estimate=pl.CostEstimate(flops=micros * 1150000000, bytes_accessed=1000, transcendentals=0),
    )(*arrays, *after)


def shift(array, step):
    return lax.ppermute(array, "z", [(i, (i + step) % 8) for i in range(8)])


def local(
    video_query,
    video_key,
    video_value,
    cross_query,
    text_key,
    text_value,
    text_mask,
    norm_gains,
    gate_table,
    timestep,
):
    bf16, f32 = jnp.bfloat16, jnp.float32
    (sums,) = call(
        sums_kernel, [((8, ROWS), f32, pltpu.VMEM)], [video_query, video_key, cross_query, text_key]
    )
    part = sums + lax.ppermute(sums, "head", [(0, 1), (1, 0), (2, 3), (3, 2)])
    other = lax.ppermute(part, "head", [(0, 2), (2, 0), (1, 3), (3, 1)])
    own, text_own = call(
        key_kernel,
        [((2 * ROWS + 16, COLS), bf16, jax.ShapeDtypeStruct), ((16, COLS), bf16, jax.ShapeDtypeStruct)],
        [text_mask, video_key, video_value, text_key, text_value, norm_gains],
        [part, other],
        1,
    )
    up1, down1 = gate([shift(own, 1), shift(own, -1)])
    (queries,) = call(
        query_kernel, [((GROUP, ROWS, COLS), bf16, pltpu.HBM)], [video_query, norm_gains], [part, other]
    )
    queries = lax.all_to_all(queries, ("y", "xh"), 0, 0)
    up2, down2 = gate([shift(up1, 1), shift(down1, -1)], micros=2)
    text4 = shift(text_own, 4)
    up3, down3 = gate([shift(up2, 1), shift(down2, -1)], after=[queries, text4], micros=2)
    (far,) = gate([shift(up3, 1)])

    ring = [own, up1, up2, up3, down1, down2, down3]
    (text,) = call(
        text_kernel,
        [((GROUP, ROWS, COLS), bf16, pltpu.HBM)],
        [],
        free=[(array, (16, COLS), (16, 0)) for array in ring] + [(text4, (16, COLS), (0, 0))],
    )
    text = lax.all_to_all(text, ("y", "xh"), 0, 0)

    (partial,) = flash_call(queries, ring + [far])

    received = lax.all_to_all(partial, ("y", "xh"), 0, 0)
    gating = lax.dynamic_slice_in_dim(gate_table, timestep[0], 1, 0)
    (cross,) = call(
        cross_kernel, [((ROWS, COLS), f32, pltpu.VMEM)], [text, cross_query, norm_gains], [part, other]
    )
    (out,) = call(final_kernel, [((ROWS, COLS), bf16, pltpu.HBM)], [received], [cross, gating])
    return out


def solution(mesh):
    grid = Mesh(mesh.devices.reshape(4, 2, 8, 4), ("y", "xh", "z", "head"))
    tokens = ("y", "xh", "z")
    placed = (
        P(tokens, "head"),
        P(tokens, "head"),
        P(tokens, "head"),
        P(tokens, "head"),
        P(tokens, "head"),
        P(tokens, "head"),
        P(tokens),
        P(None, "head"),
        P(None, "head"),
        P(),
    )
    return jax.shard_map(
        local, mesh=grid, in_specs=placed, out_specs=P(tokens, "head"), check_vma=False
    )
```

```python
import jax
import jax.numpy as jnp
from jax import lax
from jax.experimental import pallas as pl
from jax.experimental.pallas import tpu as pltpu
from jax.sharding import Mesh, PartitionSpec as P

HEADS = 20
HD = 128
LOG2E = 1.4426950408889634
SCALE2 = HD ** (-0.5) * LOG2E
PAD_MARK = 1e30
PAD_TEST = 1e20
NEG_FILL = -1e30
ROWS = 128
COLS = 640
HPD = 5
GROUP = 8
OUT_ROWS = COLS + 16
MIB = 1024 * 1024
SPAN = 256
PIECE = 32
PARTS = 1024 // SPAN
UNITS = HPD * PARTS

VM = pl.BlockSpec(memory_space=pltpu.VMEM)


def dot(a, b, ca, cb):
    return lax.dot_general(a, b, (((ca,), (cb,)), ((), ())), preferred_element_type=jnp.float32)


def thirds(value):
    hi = value.astype(jnp.bfloat16).astype(jnp.float32)
    rest = value - hi
    mid = rest.astype(jnp.bfloat16).astype(jnp.float32)
    return hi, mid, rest - mid


def columns_of(row):
    return jnp.broadcast_to(row, (ROWS, ROWS)).T


def factor_of(row):
    return lax.rsqrt(columns_of(row) * (1.0 / (HEADS * HD)) + 1e-06)


def sums_kernel(q_ref, k_ref, c_ref, t_ref, out_ref):
    lane = lax.broadcasted_iota(jnp.int32, (ROWS, ROWS), 1)
    table = jnp.zeros((ROWS, ROWS), jnp.float32)
    for n, ref in enumerate((q_ref, k_ref, c_ref)):
        values = ref[...].astype(jnp.float32)
        table = jnp.where(lane == n, jnp.sum(values * values, axis=1, keepdims=True), table)
    table = table.T
    values = t_ref[...].astype(jnp.float32)
    text = jnp.sum(values * values, axis=1, keepdims=True)
    text = jnp.where(lax.broadcasted_iota(jnp.int32, (8, ROWS), 1) == 0, text, 0.0)
    text = jnp.concatenate([text, jnp.zeros((ROWS - 8, ROWS), jnp.float32)], axis=0).T
    row = lax.broadcasted_iota(jnp.int32, (8, ROWS), 0)
    out_ref[...] = jnp.where(row == 3, text[0:1], table[0:8])


def norm_kernel(
    mask_ref, k_ref, v_ref, tk_ref, tv_ref, q_ref, gains_ref, part_ref, other_ref, out_ref, text_out, q_out
):
    sums = part_ref[...] + other_ref[...]
    q_factor = factor_of(sums[0:1])
    k_factor = factor_of(sums[1:2])
    t_factor = factor_of(sums[3:4])[0:8]
    row = lax.broadcasted_iota(jnp.int32, (8, ROWS), 0)
    usable = jnp.zeros((8, ROWS), jnp.int32)
    for n in range(8):
        usable = jnp.where(row == n, mask_ref[n], usable)
    for h in range(HPD):
        cols = slice(h * HD, (h + 1) * HD)
        k = k_ref[:, cols].astype(jnp.float32) * k_factor * gains_ref[1:2, cols]
        out_ref[0:ROWS, cols] = k.astype(jnp.bfloat16)
        t = tk_ref[:, cols].astype(jnp.float32) * t_factor * gains_ref[3:4, cols]
        t = jnp.where(usable > 0, t, PAD_MARK)
        text = jnp.concatenate([t, tv_ref[:, cols].astype(jnp.float32)], axis=0).astype(jnp.bfloat16)
        out_ref[2 * ROWS:2 * ROWS + 16, cols] = text
        text_out[:, cols] = text
        q = (q_ref[:, cols].astype(jnp.float32) * q_factor * gains_ref[0:1, cols]).astype(jnp.bfloat16)
        for j in range(GROUP):
            q_out[j, :, cols] = q
    out_ref[ROWS:2 * ROWS, :] = v_ref[...]


def text_kernel(*refs):
    parts = [ref[...].astype(jnp.float32) for ref in refs[:5]]
    parts += [ref[2 * ROWS:2 * ROWS + 16, :].astype(jnp.float32) for ref in refs[5:7]]
    parts.append(refs[7][...].astype(jnp.float32))
    out_ref = refs[8]
    keys = jnp.concatenate([part[0:8] for part in parts], axis=0).astype(jnp.bfloat16)
    values = jnp.concatenate([part[8:16] for part in parts], axis=0).astype(jnp.bfloat16)
    for j in range(GROUP):
        out_ref[j, 0:64, :] = keys
        out_ref[j, 64:128, :] = values


def unit_place(unit):
    unit = jnp.clip(unit, 0, UNITS - 1)
    head = lax.div(unit, PARTS)
    first = lax.rem(unit, PARTS) * (SPAN // ROWS)
    return head, first, pl.ds(pl.multiple_of(head * HD, HD), HD)


def flash_kernel(q_ref, *refs):
    c_refs = refs[:8]
    out_ref = refs[8]
    k_s, v_s, s_a, s_b, p_a, p_b, i_a, i_b, stat_s = refs[9:]
    lane = lax.broadcasted_iota(jnp.int32, (PIECE, ROWS), 1)
    stat_s[...] = jnp.zeros_like(stat_s)
    for n in range(8):
        rows = slice(n * ROWS, (n + 1) * ROWS)
        k_s[rows, :] = c_refs[n][0:ROWS, :]
        v_s[rows, :] = c_refs[n][ROWS:2 * ROWS, :]

    def score(unit, s_ref, tile):
        _, first, cols = unit_place(unit)
        q = q_ref[pl.ds(first, SPAN // ROWS), :, cols].reshape(SPAN, HD)
        keys = slice(tile * 256, (tile + 1) * 256)
        s_ref[:, keys] = dot(q, k_s[keys, cols], 1, 1)

    def soften(unit, s_ref, p_ref, i_ref, piece):
        head, first, _ = unit_place(unit)
        rows = slice(piece * PIECE, (piece + 1) * PIECE)
        s = s_ref[rows, :]
        top = s[:, 0:ROWS]
        for n in range(1, 8):
            top = jnp.maximum(top, s[:, n * ROWS:(n + 1) * ROWS])
        top = jnp.max(top, axis=1, keepdims=True)
        p = jnp.exp2((s - top) * SCALE2)
        total = p[:, 0:ROWS]
        for n in range(1, 8):
            total = total + p[:, n * ROWS:(n + 1) * ROWS]
        total = jnp.sum(total, axis=1, keepdims=True)
        p_ref[rows, :] = p.astype(jnp.bfloat16)
        i_ref[rows, :] = jnp.broadcast_to(1.0 / total, (PIECE, ROWS))
        hi, mid, low = thirds(jnp.broadcast_to(top * SCALE2 + jnp.log2(total), (PIECE, ROWS)))
        slot = first + piece * PIECE // ROWS
        inner = slice(piece * PIECE % ROWS, piece * PIECE % ROWS + PIECE)
        stats = jnp.where(lane == 3 * head, hi, stat_s[slot, inner, :])
        stats = jnp.where(lane == 3 * head + 1, mid, stats)
        stat_s[slot, inner, :] = jnp.where(lane == 3 * head + 2, low, stats)

    def blend(unit, p_ref, i_ref):
        head, first, cols = unit_place(unit)
        o = (dot(p_ref[...], v_s[:, cols], 1, 0) * i_ref[...]).astype(jnp.bfloat16)
        for n in range(SPAN // ROWS):
            out_ref[first + n, pl.ds(pl.multiple_of(head * HD, HD), HD), :] = o[n * ROWS:(n + 1) * ROWS]

    def phase(unit, s_next, s_now, p_now, i_now, p_last, i_last):
        blend(unit - 1, p_last, i_last)
        pieces = SPAN // PIECE
        for piece in range(pieces):
            if piece % (pieces // 4) == 0:
                score(unit + 1, s_next, piece // (pieces // 4))
            soften(unit, s_now, p_now, i_now, piece)

    for tile in range(4):
        score(0, s_a, tile)

    def step(i, carry):
        phase(2 * i, s_b, s_a, p_a, i_a, p_b, i_b)
        phase(2 * i + 1, s_a, s_b, p_b, i_b, p_a, i_a)
        return carry

    lax.fori_loop(0, UNITS // 2, step, 0)
    blend(UNITS - 1, p_b, i_b)
    for slot in range(GROUP):
        out_ref[slot, COLS:OUT_ROWS, :] = stat_s[slot].T[0:16].astype(jnp.bfloat16)


def cross_kernel(text_ref, c_ref, gains_ref, part_ref, other_ref, out_ref):
    factor = factor_of(part_ref[2:3] + other_ref[2:3])
    for h in range(HPD):
        cols = slice(h * HD, (h + 1) * HD)
        queries = (c_ref[:, cols].astype(jnp.float32) * factor * gains_ref[2:3, cols]).astype(jnp.bfloat16)
        keys = jnp.concatenate([text_ref[j, 0:64, cols] for j in range(GROUP)], axis=0)
        values = jnp.concatenate([text_ref[j, 64:128, cols] for j in range(GROUP)], axis=0)
        s = dot(keys, queries, 1, 1)
        real = keys[:, 0:1].astype(jnp.float32) < PAD_TEST
        s = jnp.where(real, s, NEG_FILL)
        top = jnp.max(s, axis=0, keepdims=True)
        p = jnp.where(real, jnp.exp2((s - top) * SCALE2), 0.0)
        total = jnp.sum(p, axis=0, keepdims=True)
        cross = dot(values, p.astype(jnp.bfloat16), 0, 0) * (1.0 / total)
        out_ref[:, cols] = cross.T


def final_kernel(in_ref, cross_ref, gate_ref, out_ref):
    for h in range(HPD):
        cols = slice(h * HD, (h + 1) * HD)
        levels = []
        for j in range(GROUP):
            stats = in_ref[j, COLS:OUT_ROWS, :].astype(jnp.float32)
            levels.append(stats[3 * h:3 * h + 1] + stats[3 * h + 1:3 * h + 2] + stats[3 * h + 2:3 * h + 3])
        top = levels[0]
        for level in levels[1:]:
            top = jnp.maximum(top, level)
        shares = [jnp.exp2(level - top) for level in levels]
        total = shares[0]
        for share in shares[1:]:
            total = total + share
        inverse = 1.0 / total
        shares = jnp.concatenate([share * inverse for share in shares], axis=0)
        shares = jnp.concatenate([shares, jnp.zeros((ROWS - GROUP, ROWS), jnp.float32)], axis=0).T
        own = jnp.zeros((ROWS, HD), jnp.float32)
        for j in range(GROUP):
            own = own + in_ref[j, h * HD:(h + 1) * HD, :].astype(jnp.float32) * shares[:, j:j + 1]
        out_ref[:, cols] = (gate_ref[:, cols] * own + cross_ref[:, cols]).astype(jnp.bfloat16)


def in_hbm(array):
    return pltpu.with_memory_space_constraint(array, pltpu.HBM)


def in_vmem(array):
    return pltpu.with_memory_space_constraint(array, pltpu.VMEM)


def block(shape, index=None):
    place = (0,) * len(shape) if index is None else index
    return pl.BlockSpec(shape, lambda i: place, pipeline_mode=pl.Buffered(buffer_count=1))


def call(kernel, shapes, arrays, near=(), scalars=0, scratch=(), cost=None, free=(), limit=60):
    ins, specs = [], []
    for n, array in enumerate(arrays):
        ins.append(array if n < scalars else in_hbm(array))
        specs.append(pl.BlockSpec(memory_space=pltpu.SMEM) if n < scalars else block(array.shape))
    for array, shape, index in free:
        ins.append(in_hbm(array) if limit < 60 else array)
        specs.append(block(shape, index))
    for array in near:
        ins.append(in_vmem(array))
        specs.append(VM)
    out_shape, out_specs = [], []
    for shape, dtype, place in shapes:
        out_shape.append(place(shape, dtype))
        out_specs.append(VM if place is pltpu.VMEM else block(shape))
    return pl.pallas_call(
        kernel,
        grid=(1,),
        out_shape=out_shape,
        in_specs=specs,
        out_specs=out_specs,
        scratch_shapes=list(scratch),
        compiler_params=pltpu.CompilerParams(vmem_limit_bytes=limit * MIB),
        cost_estimate=cost,
    )(*ins)


def flash_call(queries, ring):
    bf16, f32 = jnp.bfloat16, jnp.float32
    return call(
        flash_kernel,
        [((GROUP, OUT_ROWS, ROWS), bf16, pltpu.HBM)],
        [queries],
        ring[7:],
        0,
        [
            pltpu.VMEM((1024, COLS), bf16),
            pltpu.VMEM((1024, COLS), bf16),
            pltpu.VMEM((SPAN, 1024), f32),
            pltpu.VMEM((SPAN, 1024), f32),
            pltpu.VMEM((SPAN, 1024), bf16),
            pltpu.VMEM((SPAN, 1024), bf16),
            pltpu.VMEM((SPAN, ROWS), f32),
            pltpu.VMEM((SPAN, ROWS), f32),
            pltpu.VMEM((GROUP, ROWS, ROWS), f32),
        ],
        pl.CostEstimate(flops=15000000000, bytes_accessed=8000000, transcendentals=5242880),
        [(array, (2 * ROWS, COLS), (0, 0)) for array in ring[:7]],
        40,
    )


def pass_kernel(*refs):
    pass


def gate(arrays, after=(), micros=10):
    arrays, after = list(arrays), list(after)
    return pl.pallas_call(
        pass_kernel,
        out_shape=[jax.ShapeDtypeStruct(array.shape, array.dtype) for array in arrays],
        in_specs=[pl.BlockSpec(memory_space=pl.ANY)] * (len(arrays) + len(after)),
        out_specs=[pl.BlockSpec(memory_space=pl.ANY)] * len(arrays),
        input_output_aliases={n: n for n in range(len(arrays))},
        compiler_params=pltpu.CompilerParams(vmem_limit_bytes=MIB),
        cost_estimate=pl.CostEstimate(flops=micros * 1150000000, bytes_accessed=1000, transcendentals=0),
    )(*arrays, *after)


def shift(array, step):
    return lax.ppermute(array, "z", [(i, (i + step) % 8) for i in range(8)])


def local(
    video_query,
    video_key,
    video_value,
    cross_query,
    text_key,
    text_value,
    text_mask,
    norm_gains,
    gate_table,
    timestep,
):
    bf16, f32 = jnp.bfloat16, jnp.float32
    (sums,) = call(
        sums_kernel, [((8, ROWS), f32, pltpu.VMEM)], [video_query, video_key, cross_query, text_key]
    )
    part = sums + lax.ppermute(sums, "head", [(0, 1), (1, 0), (2, 3), (3, 2)])
    other = lax.ppermute(part, "head", [(0, 2), (2, 0), (1, 3), (3, 1)])
    own, text_own, queries = call(
        norm_kernel,
        [
            ((2 * ROWS + 16, COLS), bf16, jax.ShapeDtypeStruct),
            ((16, COLS), bf16, jax.ShapeDtypeStruct),
            ((GROUP, ROWS, COLS), bf16, pltpu.HBM),
        ],
        [text_mask, video_key, video_value, text_key, text_value, video_query, norm_gains],
        [part, other],
        1,
    )
    up1, down1 = gate([shift(own, 1), shift(own, -1)])
    queries = lax.all_to_all(queries, ("y", "xh"), 0, 0)
    up2, down2 = gate([shift(up1, 1), shift(down1, -1)], micros=2)
    text4 = shift(text_own, 4)
    up3, down3 = gate([shift(up2, 1), shift(down2, -1)], after=[queries, text4], micros=2)
    (far,) = gate([shift(up3, 1)])

    ring = [own, up1, up2, up3, down1, down2, down3]
    (text,) = call(
        text_kernel,
        [((GROUP, ROWS, COLS), bf16, pltpu.HBM)],
        [],
        [up3, down3, text4],
        free=[(array, (16, COLS), (16, 0)) for array in (own, up1, up2, down1, down2)],
        limit=16,
    )
    text = lax.all_to_all(text, ("y", "xh"), 0, 0)

    (partial,) = flash_call(queries, ring + [far])

    received = lax.all_to_all(partial, ("y", "xh"), 0, 0)
    gating = lax.dynamic_slice_in_dim(gate_table, timestep[0], 1, 0)
    (cross,) = call(
        cross_kernel, [((ROWS, COLS), f32, pltpu.VMEM)], [text, cross_query, norm_gains], [part, other]
    )
    (out,) = call(final_kernel, [((ROWS, COLS), bf16, pltpu.HBM)], [received], [cross, gating])
    return out


def solution(mesh):
    grid = Mesh(mesh.devices.reshape(4, 2, 8, 4), ("y", "xh", "z", "head"))
    tokens = ("y", "xh", "z")
    placed = (
        P(tokens, "head"),
        P(tokens, "head"),
        P(tokens, "head"),
        P(tokens, "head"),
        P(tokens, "head"),
        P(tokens, "head"),
        P(tokens),
        P(None, "head"),
        P(None, "head"),
        P(),
    )
    return jax.shard_map(
        local, mesh=grid, in_specs=placed, out_specs=P(tokens, "head"), check_vma=False
    )
```

```python
import jax
import jax.numpy as jnp
from jax import lax
from jax.experimental import pallas as pl
from jax.experimental.pallas import tpu as pltpu
from jax.sharding import Mesh, PartitionSpec as P

HEADS = 20
HD = 128
LOG2E = 1.4426950408889634
SCALE2 = HD ** (-0.5) * LOG2E
PAD_MARK = 1e30
PAD_TEST = 1e20
NEG_FILL = -1e30
ROWS = 128
COLS = 640
HPD = 5
GROUP = 8
OUT_ROWS = COLS + 16
MIB = 1024 * 1024
SPAN = 256
PIECE = 32
PARTS = 1024 // SPAN
UNITS = HPD * PARTS

VM = pl.BlockSpec(memory_space=pltpu.VMEM)


def dot(a, b, ca, cb):
    return lax.dot_general(a, b, (((ca,), (cb,)), ((), ())), preferred_element_type=jnp.float32)


def thirds(value):
    hi = value.astype(jnp.bfloat16).astype(jnp.float32)
    rest = value - hi
    mid = rest.astype(jnp.bfloat16).astype(jnp.float32)
    return hi, mid, rest - mid


def columns_of(row):
    return jnp.broadcast_to(row, (ROWS, ROWS)).T


def factor_of(row):
    return lax.rsqrt(columns_of(row) * (1.0 / (HEADS * HD)) + 1e-06)


def sums_kernel(q_ref, k_ref, c_ref, t_ref, out_ref):
    lane = lax.broadcasted_iota(jnp.int32, (ROWS, ROWS), 1)
    table = jnp.zeros((ROWS, ROWS), jnp.float32)
    for n, ref in enumerate((q_ref, k_ref, c_ref)):
        values = ref[...].astype(jnp.float32)
        table = jnp.where(lane == n, jnp.sum(values * values, axis=1, keepdims=True), table)
    table = table.T
    values = t_ref[...].astype(jnp.float32)
    text = jnp.sum(values * values, axis=1, keepdims=True)
    text = jnp.where(lax.broadcasted_iota(jnp.int32, (8, ROWS), 1) == 0, text, 0.0)
    text = jnp.concatenate([text, jnp.zeros((ROWS - 8, ROWS), jnp.float32)], axis=0).T
    row = lax.broadcasted_iota(jnp.int32, (8, ROWS), 0)
    out_ref[...] = jnp.where(row == 3, text[0:1], table[0:8])


def norm_kernel(
    mask_ref, k_ref, v_ref, tk_ref, tv_ref, q_ref, gains_ref, part_ref, other_ref, out_ref, q_out
):
    sums = part_ref[...] + other_ref[...]
    q_factor = factor_of(sums[0:1])
    k_factor = factor_of(sums[1:2])
    t_factor = factor_of(sums[3:4])[0:8]
    row = lax.broadcasted_iota(jnp.int32, (8, ROWS), 0)
    usable = jnp.zeros((8, ROWS), jnp.int32)
    for n in range(8):
        usable = jnp.where(row == n, mask_ref[n], usable)
    for h in range(HPD):
        cols = slice(h * HD, (h + 1) * HD)
        k = k_ref[:, cols].astype(jnp.float32) * k_factor * gains_ref[1:2, cols]
        out_ref[0:ROWS, cols] = k.astype(jnp.bfloat16)
        t = tk_ref[:, cols].astype(jnp.float32) * t_factor * gains_ref[3:4, cols]
        t = jnp.where(usable > 0, t, PAD_MARK)
        text = jnp.concatenate([t, tv_ref[:, cols].astype(jnp.float32)], axis=0).astype(jnp.bfloat16)
        out_ref[2 * ROWS:2 * ROWS + 16, cols] = text
        q = (q_ref[:, cols].astype(jnp.float32) * q_factor * gains_ref[0:1, cols]).astype(jnp.bfloat16)
        for j in range(GROUP):
            q_out[j, :, cols] = q
    out_ref[ROWS:2 * ROWS, :] = v_ref[...]


def pick_kernel(own_ref, near_up_ref, near_down_ref, down_ref, up_ref, picked_ref, pass_ref):
    parts = [ref[...].astype(jnp.float32) for ref in (own_ref, near_up_ref, near_down_ref, down_ref)]
    up = up_ref[...]
    pass_ref[...] = up
    parts.append(up.astype(jnp.float32))
    parts.append(jnp.zeros_like(parts[0]))
    picked_ref[0:48, :] = jnp.concatenate([part[0:8] for part in parts], axis=0).astype(jnp.bfloat16)
    picked_ref[48:96, :] = jnp.concatenate([part[8:16] for part in parts], axis=0).astype(jnp.bfloat16)


def text_kernel(picked_ref, far_ref, up_ref, down_ref, out_ref):
    parts = [far_ref[...].astype(jnp.float32)]
    for ref in (up_ref, down_ref):
        parts.append(ref[2 * ROWS:2 * ROWS + 16, :].astype(jnp.float32))
    keys = jnp.concatenate([picked_ref[32:48, :].astype(jnp.float32)[0:8]] + [part[0:8] for part in parts], axis=0)
    values = jnp.concatenate([picked_ref[80:96, :].astype(jnp.float32)[0:8]] + [part[8:16] for part in parts], axis=0)
    for j in range(GROUP):
        out_ref[j, 0:32, :] = picked_ref[0:32, :]
        out_ref[j, 32:64, :] = keys.astype(jnp.bfloat16)
        out_ref[j, 64:96, :] = picked_ref[48:80, :]
        out_ref[j, 96:128, :] = values.astype(jnp.bfloat16)


def unit_place(unit):
    unit = jnp.clip(unit, 0, UNITS - 1)
    head = lax.div(unit, PARTS)
    first = lax.rem(unit, PARTS) * (SPAN // ROWS)
    return head, first, pl.ds(pl.multiple_of(head * HD, HD), HD)


def flash_kernel(q_ref, *refs):
    c_refs = refs[:8]
    out_ref = refs[8]
    k_s, v_s, s_a, s_b, p_a, p_b, i_a, i_b, stat_s = refs[9:]
    lane = lax.broadcasted_iota(jnp.int32, (PIECE, ROWS), 1)
    stat_s[...] = jnp.zeros_like(stat_s)
    for n in range(8):
        rows = slice(n * ROWS, (n + 1) * ROWS)
        k_s[rows, :] = c_refs[n][0:ROWS, :]
        v_s[rows, :] = c_refs[n][ROWS:2 * ROWS, :]

    def score(unit, s_ref, tile):
        _, first, cols = unit_place(unit)
        q = q_ref[pl.ds(first, SPAN // ROWS), :, cols].reshape(SPAN, HD)
        keys = slice(tile * 256, (tile + 1) * 256)
        s_ref[:, keys] = dot(q, k_s[keys, cols], 1, 1)

    def soften(unit, s_ref, p_ref, i_ref, piece):
        head, first, _ = unit_place(unit)
        rows = slice(piece * PIECE, (piece + 1) * PIECE)
        s = s_ref[rows, :]
        top = s[:, 0:ROWS]
        for n in range(1, 8):
            top = jnp.maximum(top, s[:, n * ROWS:(n + 1) * ROWS])
        top = jnp.max(top, axis=1, keepdims=True)
        p = jnp.exp2((s - top) * SCALE2)
        total = p[:, 0:ROWS]
        for n in range(1, 8):
            total = total + p[:, n * ROWS:(n + 1) * ROWS]
        total = jnp.sum(total, axis=1, keepdims=True)
        p_ref[rows, :] = p.astype(jnp.bfloat16)
        i_ref[rows, :] = jnp.broadcast_to(1.0 / total, (PIECE, ROWS))
        hi, mid, low = thirds(jnp.broadcast_to(top * SCALE2 + jnp.log2(total), (PIECE, ROWS)))
        slot = first + piece * PIECE // ROWS
        inner = slice(piece * PIECE % ROWS, piece * PIECE % ROWS + PIECE)
        stats = jnp.where(lane == 3 * head, hi, stat_s[slot, inner, :])
        stats = jnp.where(lane == 3 * head + 1, mid, stats)
        stat_s[slot, inner, :] = jnp.where(lane == 3 * head + 2, low, stats)

    def blend(unit, p_ref, i_ref):
        head, first, cols = unit_place(unit)
        o = (dot(p_ref[...], v_s[:, cols], 1, 0) * i_ref[...]).T.astype(jnp.bfloat16)
        for n in range(SPAN // ROWS):
            out_ref[first + n, pl.ds(pl.multiple_of(head * HD, HD), HD), :] = o[:, n * ROWS:(n + 1) * ROWS]

    def phase(unit, s_next, s_now, p_now, i_now, p_last, i_last):
        blend(unit - 1, p_last, i_last)
        pieces = SPAN // PIECE
        for piece in range(pieces):
            if piece % (pieces // 4) == 0:
                score(unit + 1, s_next, piece // (pieces // 4))
            soften(unit, s_now, p_now, i_now, piece)

    for tile in range(4):
        score(0, s_a, tile)

    def step(i, carry):
        phase(2 * i, s_b, s_a, p_a, i_a, p_b, i_b)
        phase(2 * i + 1, s_a, s_b, p_b, i_b, p_a, i_a)
        return carry

    lax.fori_loop(0, UNITS // 2, step, 0)
    blend(UNITS - 1, p_b, i_b)
    for slot in range(GROUP):
        out_ref[slot, COLS:OUT_ROWS, :] = stat_s[slot].T[0:16].astype(jnp.bfloat16)


def cross_kernel(text_ref, c_ref, gains_ref, part_ref, other_ref, out_ref):
    factor = factor_of(part_ref[2:3] + other_ref[2:3])
    for h in range(HPD):
        cols = slice(h * HD, (h + 1) * HD)
        queries = (c_ref[:, cols].astype(jnp.float32) * factor * gains_ref[2:3, cols]).astype(jnp.bfloat16)
        keys = jnp.concatenate([text_ref[j, 0:64, cols] for j in range(GROUP)], axis=0)
        values = jnp.concatenate([text_ref[j, 64:128, cols] for j in range(GROUP)], axis=0)
        s = dot(keys, queries, 1, 1)
        real = keys[:, 0:1].astype(jnp.float32) < PAD_TEST
        s = jnp.where(real, s, NEG_FILL)
        top = jnp.max(s, axis=0, keepdims=True)
        p = jnp.where(real, jnp.exp2((s - top) * SCALE2), 0.0)
        total = jnp.sum(p, axis=0, keepdims=True)
        cross = dot(values, p.astype(jnp.bfloat16), 0, 0) * (1.0 / total)
        out_ref[:, cols] = cross.T


def final_kernel(in_ref, cross_ref, gate_ref, out_ref):
    for h in range(HPD):
        cols = slice(h * HD, (h + 1) * HD)
        levels = []
        for j in range(GROUP):
            stats = in_ref[j, COLS:OUT_ROWS, :].astype(jnp.float32)
            levels.append(stats[3 * h:3 * h + 1] + stats[3 * h + 1:3 * h + 2] + stats[3 * h + 2:3 * h + 3])
        top = levels[0]
        for level in levels[1:]:
            top = jnp.maximum(top, level)
        shares = [jnp.exp2(level - top) for level in levels]
        total = shares[0]
        for share in shares[1:]:
            total = total + share
        inverse = 1.0 / total
        own = jnp.zeros((HD, ROWS), jnp.float32)
        for j in range(GROUP):
            own = own + in_ref[j, h * HD:(h + 1) * HD, :].astype(jnp.float32) * (shares[j] * inverse)
        out_ref[:, cols] = (gate_ref[:, cols] * own.T + cross_ref[:, cols]).astype(jnp.bfloat16)


def in_hbm(array):
    return pltpu.with_memory_space_constraint(array, pltpu.HBM)


def in_vmem(array):
    return pltpu.with_memory_space_constraint(array, pltpu.VMEM)


def block(shape, index=None):
    place = (0,) * len(shape) if index is None else index
    return pl.BlockSpec(shape, lambda i: place, pipeline_mode=pl.Buffered(buffer_count=1))


def call(kernel, shapes, arrays, near=(), scalars=0, scratch=(), cost=None, free=(), limit=60):
    ins, specs = [], []
    for n, array in enumerate(arrays):
        ins.append(array if n < scalars else in_hbm(array))
        specs.append(pl.BlockSpec(memory_space=pltpu.SMEM) if n < scalars else block(array.shape))
    for array, shape, index in free:
        ins.append(in_hbm(array) if limit < 60 else array)
        specs.append(block(shape, index))
    for array in near:
        ins.append(in_vmem(array))
        specs.append(VM)
    out_shape, out_specs = [], []
    for shape, dtype, place in shapes:
        out_shape.append(place(shape, dtype))
        out_specs.append(VM if place is pltpu.VMEM else block(shape))
    return pl.pallas_call(
        kernel,
        grid=(1,),
        out_shape=out_shape,
        in_specs=specs,
        out_specs=out_specs,
        scratch_shapes=list(scratch),
        compiler_params=pltpu.CompilerParams(vmem_limit_bytes=limit * MIB),
        cost_estimate=cost,
    )(*ins)


def flash_call(queries, ring):
    bf16, f32 = jnp.bfloat16, jnp.float32
    return call(
        flash_kernel,
        [((GROUP, OUT_ROWS, ROWS), bf16, pltpu.HBM)],
        [queries],
        ring[7:],
        0,
        [
            pltpu.VMEM((1024, COLS), bf16),
            pltpu.VMEM((1024, COLS), bf16),
            pltpu.VMEM((SPAN, 1024), f32),
            pltpu.VMEM((SPAN, 1024), f32),
            pltpu.VMEM((SPAN, 1024), bf16),
            pltpu.VMEM((SPAN, 1024), bf16),
            pltpu.VMEM((SPAN, ROWS), f32),
            pltpu.VMEM((SPAN, ROWS), f32),
            pltpu.VMEM((GROUP, ROWS, ROWS), f32),
        ],
        pl.CostEstimate(flops=15000000000, bytes_accessed=8000000, transcendentals=5242880),
        [(array, (2 * ROWS, COLS), (0, 0)) for array in ring[:7]],
        40,
    )


def pass_kernel(*refs):
    pass


def gate(arrays, after=(), micros=10):
    arrays, after = list(arrays), list(after)
    return pl.pallas_call(
        pass_kernel,
        out_shape=[jax.ShapeDtypeStruct(array.shape, array.dtype) for array in arrays],
        in_specs=[pl.BlockSpec(memory_space=pl.ANY)] * (len(arrays) + len(after)),
        out_specs=[pl.BlockSpec(memory_space=pl.ANY)] * len(arrays),
        input_output_aliases={n: n for n in range(len(arrays))},
        compiler_params=pltpu.CompilerParams(vmem_limit_bytes=MIB),
        cost_estimate=pl.CostEstimate(flops=micros * 1150000000, bytes_accessed=1000, transcendentals=0),
    )(*arrays, *after)


def shift(array, step):
    return lax.ppermute(array, "z", [(i, (i + step) % 8) for i in range(8)])


def local(
    video_query,
    video_key,
    video_value,
    cross_query,
    text_key,
    text_value,
    text_mask,
    norm_gains,
    gate_table,
    timestep,
):
    bf16, f32 = jnp.bfloat16, jnp.float32
    (sums,) = call(
        sums_kernel, [((8, ROWS), f32, pltpu.VMEM)], [video_query, video_key, cross_query, text_key]
    )
    part = sums + lax.ppermute(sums, "head", [(0, 1), (1, 0), (2, 3), (3, 2)])
    other = lax.ppermute(part, "head", [(0, 2), (2, 0), (1, 3), (3, 1)])
    own, queries = call(
        norm_kernel,
        [
            ((2 * ROWS + 16, COLS), bf16, jax.ShapeDtypeStruct),
            ((GROUP, ROWS, COLS), bf16, pltpu.HBM),
        ],
        [text_mask, video_key, video_value, text_key, text_value, video_query, norm_gains],
        [part, other],
        1,
    )
    up1, down1 = gate([shift(own, 1), shift(own, -1)])
    queries = lax.all_to_all(queries, ("y", "xh"), 0, 0)
    up2, down2 = gate([shift(up1, 1), shift(down1, -1)], micros=2)
    picked, passing = call(
        pick_kernel,
        [((96, COLS), bf16, jax.ShapeDtypeStruct), ((16, COLS), bf16, jax.ShapeDtypeStruct)],
        [],
        [],
        limit=16,
        free=[(array, (16, COLS), (16, 0)) for array in (own, up1, down1, down2, up2)],
    )
    text4 = shift(passing, 2)
    up3, down3 = gate([shift(up2, 1), shift(down2, -1)], after=[queries, text4], micros=2)
    (far,) = gate([shift(up3, 1)])

    ring = [own, up1, up2, up3, down1, down2, down3]
    (text,) = call(
        text_kernel, [((GROUP, ROWS, COLS), bf16, pltpu.HBM)], [], [picked, text4, up3, down3], limit=16
    )
    text = lax.all_to_all(text, ("y", "xh"), 0, 0)

    (partial,) = flash_call(queries, ring + [far])

    received = lax.all_to_all(partial, ("y", "xh"), 0, 0)
    gating = lax.dynamic_slice_in_dim(gate_table, timestep[0], 1, 0)
    (cross,) = call(
        cross_kernel, [((ROWS, COLS), f32, pltpu.VMEM)], [text, cross_query, norm_gains], [part, other]
    )
    (out,) = call(final_kernel, [((ROWS, COLS), bf16, pltpu.HBM)], [received], [cross, gating])
    return out


def solution(mesh):
    grid = Mesh(mesh.devices.reshape(4, 2, 8, 4), ("y", "xh", "z", "head"))
    tokens = ("y", "xh", "z")
    placed = (
        P(tokens, "head"),
        P(tokens, "head"),
        P(tokens, "head"),
        P(tokens, "head"),
        P(tokens, "head"),
        P(tokens, "head"),
        P(tokens),
        P(None, "head"),
        P(None, "head"),
        P(),
    )
    return jax.shard_map(
        local, mesh=grid, in_specs=placed, out_specs=P(tokens, "head"), check_vma=False
    )
```

```python
import jax
import jax.numpy as jnp
from jax import lax
from jax.experimental import pallas as pl
from jax.experimental.pallas import tpu as pltpu
from jax.sharding import Mesh, PartitionSpec as P

HEADS = 20
HD = 128
LOG2E = 1.4426950408889634
SCALE2 = HD ** (-0.5) * LOG2E
PAD_MARK = 1e30
PAD_TEST = 1e20
NEG_FILL = -1e30
ROWS = 128
COLS = 640
HPD = 5
GROUP = 8
OUT_ROWS = COLS + 16
MIB = 1024 * 1024
SPAN = 256
PIECE = 32
PARTS = 1024 // SPAN
UNITS = HPD * PARTS

VM = pl.BlockSpec(memory_space=pltpu.VMEM)


def dot(a, b, ca, cb):
    return lax.dot_general(a, b, (((ca,), (cb,)), ((), ())), preferred_element_type=jnp.float32)


def thirds(value):
    hi = value.astype(jnp.bfloat16).astype(jnp.float32)
    rest = value - hi
    mid = rest.astype(jnp.bfloat16).astype(jnp.float32)
    return hi, mid, rest - mid


def columns_of(row):
    return jnp.broadcast_to(row, (ROWS, ROWS)).T


def factor_of(row):
    return lax.rsqrt(columns_of(row) * (1.0 / (HEADS * HD)) + 1e-06)


def sums_kernel(q_ref, k_ref, c_ref, t_ref, out_ref):
    lane = lax.broadcasted_iota(jnp.int32, (ROWS, ROWS), 1)
    table = jnp.zeros((ROWS, ROWS), jnp.float32)
    for n, ref in enumerate((q_ref, k_ref, c_ref)):
        values = ref[...].astype(jnp.float32)
        table = jnp.where(lane == n, jnp.sum(values * values, axis=1, keepdims=True), table)
    table = table.T
    values = t_ref[...].astype(jnp.float32)
    text = jnp.sum(values * values, axis=1, keepdims=True)
    text = jnp.where(lax.broadcasted_iota(jnp.int32, (8, ROWS), 1) == 0, text, 0.0)
    text = jnp.concatenate([text, jnp.zeros((ROWS - 8, ROWS), jnp.float32)], axis=0).T
    row = lax.broadcasted_iota(jnp.int32, (8, ROWS), 0)
    out_ref[...] = jnp.where(row == 3, text[0:1], table[0:8])


def norm_kernel(
    mask_ref, k_ref, v_ref, tk_ref, tv_ref, q_ref, gains_ref, part_ref, other_ref, out_ref, q_out
):
    sums = part_ref[...] + other_ref[...]
    table = jnp.concatenate([sums, jnp.zeros((ROWS - 8, ROWS), jnp.float32)], axis=0).T
    factors = lax.rsqrt(table * (1.0 / (HEADS * HD)) + 1e-06)
    q_factor = jnp.broadcast_to(factors[:, 0:1], (ROWS, ROWS))
    k_factor = jnp.broadcast_to(factors[:, 1:2], (ROWS, ROWS))
    t_factor = jnp.broadcast_to(factors[0:8, 3:4], (8, ROWS))
    row = lax.broadcasted_iota(jnp.int32, (8, ROWS), 0)
    usable = jnp.zeros((8, ROWS), jnp.int32)
    for n in range(8):
        usable = jnp.where(row == n, mask_ref[n], usable)
    for h in range(HPD):
        cols = slice(h * HD, (h + 1) * HD)
        k = k_ref[:, cols].astype(jnp.float32) * k_factor * gains_ref[1:2, cols]
        out_ref[0:ROWS, cols] = k.astype(jnp.bfloat16)
        t = tk_ref[:, cols].astype(jnp.float32) * t_factor * gains_ref[3:4, cols]
        t = jnp.where(usable > 0, t, PAD_MARK)
        text = jnp.concatenate([t, tv_ref[:, cols].astype(jnp.float32)], axis=0).astype(jnp.bfloat16)
        out_ref[2 * ROWS:2 * ROWS + 16, cols] = text
        q = (q_ref[:, cols].astype(jnp.float32) * q_factor * gains_ref[0:1, cols]).astype(jnp.bfloat16)
        for j in range(GROUP):
            q_out[j, :, cols] = q
    out_ref[ROWS:2 * ROWS, :] = v_ref[...]


def pick_kernel(own_ref, near_up_ref, near_down_ref, down_ref, up_ref, picked_ref, pass_ref):
    parts = [ref[...].astype(jnp.float32) for ref in (own_ref, near_up_ref, near_down_ref, down_ref)]
    up = up_ref[...]
    pass_ref[...] = up
    parts.append(up.astype(jnp.float32))
    parts.append(jnp.zeros_like(parts[0]))
    picked_ref[0:48, :] = jnp.concatenate([part[0:8] for part in parts], axis=0).astype(jnp.bfloat16)
    picked_ref[48:96, :] = jnp.concatenate([part[8:16] for part in parts], axis=0).astype(jnp.bfloat16)


def text_kernel(picked_ref, far_ref, up_ref, down_ref, out_ref):
    parts = [far_ref[...].astype(jnp.float32)]
    for ref in (up_ref, down_ref):
        parts.append(ref[2 * ROWS:2 * ROWS + 16, :].astype(jnp.float32))
    keys = jnp.concatenate([picked_ref[32:48, :].astype(jnp.float32)[0:8]] + [part[0:8] for part in parts], axis=0)
    values = jnp.concatenate([picked_ref[80:96, :].astype(jnp.float32)[0:8]] + [part[8:16] for part in parts], axis=0)
    for j in range(GROUP):
        out_ref[j, 0:32, :] = picked_ref[0:32, :]
        out_ref[j, 32:64, :] = keys.astype(jnp.bfloat16)
        out_ref[j, 64:96, :] = picked_ref[48:80, :]
        out_ref[j, 96:128, :] = values.astype(jnp.bfloat16)


def unit_place(unit):
    unit = jnp.clip(unit, 0, UNITS - 1)
    head = lax.div(unit, PARTS)
    first = lax.rem(unit, PARTS) * (SPAN // ROWS)
    return head, first, pl.ds(pl.multiple_of(head * HD, HD), HD)


def flash_kernel(q_ref, *refs):
    c_refs = refs[:8]
    out_ref = refs[8]
    k_s, v_s, s_a, s_b, p_a, p_b, i_a, i_b, stat_s = refs[9:]
    lane = lax.broadcasted_iota(jnp.int32, (PIECE, ROWS), 1)
    stat_s[...] = jnp.zeros_like(stat_s)
    for n in range(8):
        rows = slice(n * ROWS, (n + 1) * ROWS)
        k_s[rows, :] = c_refs[n][0:ROWS, :]
        v_s[rows, :] = c_refs[n][ROWS:2 * ROWS, :]

    def score(unit, s_ref, tile):
        _, first, cols = unit_place(unit)
        q = q_ref[pl.ds(first, SPAN // ROWS), :, cols].reshape(SPAN, HD)
        keys = slice(tile * 256, (tile + 1) * 256)
        s_ref[:, keys] = dot(q, k_s[keys, cols], 1, 1)

    def soften(unit, s_ref, p_ref, i_ref, piece):
        head, first, _ = unit_place(unit)
        rows = slice(piece * PIECE, (piece + 1) * PIECE)
        s = s_ref[rows, :]
        top = s[:, 0:ROWS]
        for n in range(1, 8):
            top = jnp.maximum(top, s[:, n * ROWS:(n + 1) * ROWS])
        top = jnp.max(top, axis=1, keepdims=True)
        p = jnp.exp2((s - top) * SCALE2)
        total = p[:, 0:ROWS]
        for n in range(1, 8):
            total = total + p[:, n * ROWS:(n + 1) * ROWS]
        total = jnp.sum(total, axis=1, keepdims=True)
        p_ref[rows, :] = p.astype(jnp.bfloat16)
        i_ref[rows, :] = jnp.broadcast_to(1.0 / total, (PIECE, ROWS))
        hi, mid, low = thirds(jnp.broadcast_to(top * SCALE2 + jnp.log2(total), (PIECE, ROWS)))
        slot = first + piece * PIECE // ROWS
        inner = slice(piece * PIECE % ROWS, piece * PIECE % ROWS + PIECE)
        stats = jnp.where(lane == 3 * head, hi, stat_s[slot, inner, :])
        stats = jnp.where(lane == 3 * head + 1, mid, stats)
        stat_s[slot, inner, :] = jnp.where(lane == 3 * head + 2, low, stats)

    def blend(unit, p_ref, i_ref):
        head, first, cols = unit_place(unit)
        o = (dot(p_ref[...], v_s[:, cols], 1, 0) * i_ref[...]).T.astype(jnp.bfloat16)
        for n in range(SPAN // ROWS):
            out_ref[first + n, pl.ds(pl.multiple_of(head * HD, HD), HD), :] = o[:, n * ROWS:(n + 1) * ROWS]

    def phase(unit, s_next, s_now, p_now, i_now, p_last, i_last):
        blend(unit - 1, p_last, i_last)
        pieces = SPAN // PIECE
        for piece in range(pieces):
            if piece % (pieces // 4) == 0:
                score(unit + 1, s_next, piece // (pieces // 4))
            soften(unit, s_now, p_now, i_now, piece)

    for tile in range(4):
        score(0, s_a, tile)

    def step(i, carry):
        phase(2 * i, s_b, s_a, p_a, i_a, p_b, i_b)
        phase(2 * i + 1, s_a, s_b, p_b, i_b, p_a, i_a)
        return carry

    lax.fori_loop(0, UNITS // 2, step, 0)
    blend(UNITS - 1, p_b, i_b)
    for slot in range(GROUP):
        out_ref[slot, COLS:OUT_ROWS, :] = stat_s[slot].T[0:16].astype(jnp.bfloat16)


def cross_kernel(text_ref, c_ref, gains_ref, part_ref, other_ref, out_ref):
    factor = factor_of(part_ref[2:3] + other_ref[2:3])
    for h in range(HPD):
        cols = slice(h * HD, (h + 1) * HD)
        queries = (c_ref[:, cols].astype(jnp.float32) * factor * gains_ref[2:3, cols]).astype(jnp.bfloat16)
        keys = jnp.concatenate([text_ref[j, 0:64, cols] for j in range(GROUP)], axis=0)
        values = jnp.concatenate([text_ref[j, 64:128, cols] for j in range(GROUP)], axis=0)
        s = dot(keys, queries, 1, 1)
        real = keys[:, 0:1].astype(jnp.float32) < PAD_TEST
        s = jnp.where(real, s, NEG_FILL)
        top = jnp.max(s, axis=0, keepdims=True)
        p = jnp.where(real, jnp.exp2((s - top) * SCALE2), 0.0)
        total = jnp.sum(p, axis=0, keepdims=True)
        cross = dot(values, p.astype(jnp.bfloat16), 0, 0) * (1.0 / total)
        out_ref[:, cols] = cross.T


def final_kernel(in_ref, cross_ref, gate_ref, out_ref):
    for h in range(HPD):
        cols = slice(h * HD, (h + 1) * HD)
        levels = []
        for j in range(GROUP):
            stats = in_ref[j, COLS:OUT_ROWS, :].astype(jnp.float32)
            levels.append(stats[3 * h:3 * h + 1] + stats[3 * h + 1:3 * h + 2] + stats[3 * h + 2:3 * h + 3])
        top = levels[0]
        for level in levels[1:]:
            top = jnp.maximum(top, level)
        shares = [jnp.exp2(level - top) for level in levels]
        total = shares[0]
        for share in shares[1:]:
            total = total + share
        inverse = 1.0 / total
        own = jnp.zeros((HD, ROWS), jnp.float32)
        for j in range(GROUP):
            own = own + in_ref[j, h * HD:(h + 1) * HD, :].astype(jnp.float32) * (shares[j] * inverse)
        out_ref[:, cols] = (gate_ref[:, cols] * own.T + cross_ref[:, cols]).astype(jnp.bfloat16)


def in_hbm(array):
    return pltpu.with_memory_space_constraint(array, pltpu.HBM)


def in_vmem(array):
    return pltpu.with_memory_space_constraint(array, pltpu.VMEM)


def block(shape, index=None):
    place = (0,) * len(shape) if index is None else index
    return pl.BlockSpec(shape, lambda i: place, pipeline_mode=pl.Buffered(buffer_count=1))


def call(kernel, shapes, arrays, near=(), scalars=0, scratch=(), cost=None, free=(), limit=60):
    ins, specs = [], []
    for n, array in enumerate(arrays):
        ins.append(array if n < scalars else in_hbm(array))
        specs.append(pl.BlockSpec(memory_space=pltpu.SMEM) if n < scalars else block(array.shape))
    for array, shape, index in free:
        ins.append(in_hbm(array) if limit < 60 else array)
        specs.append(block(shape, index))
    for array in near:
        ins.append(in_vmem(array))
        specs.append(VM)
    out_shape, out_specs = [], []
    for shape, dtype, place in shapes:
        out_shape.append(place(shape, dtype))
        out_specs.append(VM if place is pltpu.VMEM else block(shape))
    return pl.pallas_call(
        kernel,
        grid=(1,),
        out_shape=out_shape,
        in_specs=specs,
        out_specs=out_specs,
        scratch_shapes=list(scratch),
        compiler_params=pltpu.CompilerParams(vmem_limit_bytes=limit * MIB),
        cost_estimate=cost,
    )(*ins)


def flash_call(queries, ring):
    bf16, f32 = jnp.bfloat16, jnp.float32
    return call(
        flash_kernel,
        [((GROUP, OUT_ROWS, ROWS), bf16, pltpu.HBM)],
        [queries],
        ring[7:],
        0,
        [
            pltpu.VMEM((1024, COLS), bf16),
            pltpu.VMEM((1024, COLS), bf16),
            pltpu.VMEM((SPAN, 1024), f32),
            pltpu.VMEM((SPAN, 1024), f32),
            pltpu.VMEM((SPAN, 1024), bf16),
            pltpu.VMEM((SPAN, 1024), bf16),
            pltpu.VMEM((SPAN, ROWS), f32),
            pltpu.VMEM((SPAN, ROWS), f32),
            pltpu.VMEM((GROUP, ROWS, ROWS), f32),
        ],
        pl.CostEstimate(flops=15000000000, bytes_accessed=8000000, transcendentals=5242880),
        [(array, (2 * ROWS, COLS), (0, 0)) for array in ring[:7]],
        40,
    )


def pass_kernel(*refs):
    pass


def gate(arrays, after=(), micros=10):
    arrays, after = list(arrays), list(after)
    return pl.pallas_call(
        pass_kernel,
        out_shape=[jax.ShapeDtypeStruct(array.shape, array.dtype) for array in arrays],
        in_specs=[pl.BlockSpec(memory_space=pl.ANY)] * (len(arrays) + len(after)),
        out_specs=[pl.BlockSpec(memory_space=pl.ANY)] * len(arrays),
        input_output_aliases={n: n for n in range(len(arrays))},
        compiler_params=pltpu.CompilerParams(vmem_limit_bytes=MIB),
        cost_estimate=pl.CostEstimate(flops=micros * 1150000000, bytes_accessed=1000, transcendentals=0),
    )(*arrays, *after)


def shift(array, step):
    return lax.ppermute(array, "z", [(i, (i + step) % 8) for i in range(8)])


def local(
    video_query,
    video_key,
    video_value,
    cross_query,
    text_key,
    text_value,
    text_mask,
    norm_gains,
    gate_table,
    timestep,
):
    bf16, f32 = jnp.bfloat16, jnp.float32
    (sums,) = call(
        sums_kernel, [((8, ROWS), f32, pltpu.VMEM)], [video_query, video_key, cross_query, text_key]
    )
    beside = lax.ppermute(sums, "head", [(0, 1), (1, 0), (2, 3), (3, 2)])
    across = lax.ppermute(sums, "head", [(0, 2), (2, 0), (1, 3), (3, 1)])
    corner = lax.ppermute(sums, "head", [(0, 3), (3, 0), (1, 2), (2, 1)])
    part, other = sums + beside, across + corner
    own, queries = call(
        norm_kernel,
        [
            ((2 * ROWS + 16, COLS), bf16, jax.ShapeDtypeStruct),
            ((GROUP, ROWS, COLS), bf16, pltpu.HBM),
        ],
        [text_mask, video_key, video_value, text_key, text_value, video_query, norm_gains],
        [part, other],
        1,
    )
    up1, down1 = gate([shift(own, 1), shift(own, -1)])
    queries = lax.all_to_all(queries, ("y", "xh"), 0, 0)
    up2, down2 = gate([shift(up1, 1), shift(down1, -1)], micros=2)
    picked, passing = call(
        pick_kernel,
        [((96, COLS), bf16, jax.ShapeDtypeStruct), ((16, COLS), bf16, jax.ShapeDtypeStruct)],
        [],
        [],
        limit=16,
        free=[(array, (16, COLS), (16, 0)) for array in (own, up1, down1, down2, up2)],
    )
    text4 = shift(passing, 2)
    up3, down3 = gate([shift(up2, 1), shift(down2, -1)], after=[queries, text4], micros=2)
    (far,) = gate([shift(up3, 1)])

    ring = [own, up1, up2, up3, down1, down2, down3]
    (text,) = call(
        text_kernel, [((GROUP, ROWS, COLS), bf16, pltpu.HBM)], [], [picked, text4, up3, down3], limit=16
    )
    text = lax.all_to_all(text, ("y", "xh"), 0, 0)

    (partial,) = flash_call(queries, ring + [far])

    received = lax.all_to_all(partial, ("y", "xh"), 0, 0)
    gating = lax.dynamic_slice_in_dim(gate_table, timestep[0], 1, 0)
    (cross,) = call(
        cross_kernel, [((ROWS, COLS), f32, pltpu.VMEM)], [text, cross_query, norm_gains], [part, other]
    )
    (out,) = call(final_kernel, [((ROWS, COLS), bf16, pltpu.HBM)], [received], [cross, gating])
    return out


def solution(mesh):
    grid = Mesh(mesh.devices.reshape(4, 2, 8, 4), ("y", "xh", "z", "head"))
    tokens = ("y", "xh", "z")
    placed = (
        P(tokens, "head"),
        P(tokens, "head"),
        P(tokens, "head"),
        P(tokens, "head"),
        P(tokens, "head"),
        P(tokens, "head"),
        P(tokens),
        P(None, "head"),
        P(None, "head"),
        P(),
    )
    return jax.shard_map(
        local, mesh=grid, in_specs=placed, out_specs=P(tokens, "head"), check_vma=False
    )
```
